32 devices in a mesh: groups: 2 (over y), blk: 16 (over z, x, core).
Axes of the slice: x: 2, y: 2, z: 4, core: 2. Of those that a mesh axis runs over, the one named last changes fastest.
Arguments:
- particles: bfloat16 [4096, 32, 256], P(('groups', 'blk')), parts along dimension 0, may hold values from -6 to 6
- owner: int32 [4096, 1], P(('groups', 'blk')), parts along dimension 0, may hold values from 0 to 15; in each aligned block of 128 rows (0 to 127, 128 to 255, ...) at most 12 rows name the same one
- mic_local: int32 [4096], P(('groups', 'blk')), parts along dimension 0, may hold values from 0 to 5
- shifts: int32 [4096, 2], P(('groups', 'blk')), parts along dimension 0, may hold values from -5 to 5
- prior: int32 [4096], P(('groups', 'blk')), parts along dimension 0, may hold values from 0 to 9
- refs: bfloat16 [32, 32, 256], P(('groups', 'blk')), parts along dimension 0, may hold values from -8 to 8
- ctf: bfloat16 [192, 32, 128], P(('groups', 'blk')), parts along dimension 0, may hold values from -1 to 1
Outputs:
- posterior: float32 [4096, 16], P(('groups', 'blk')), parts along dimension 0
- evidence: float32 [4096], P(('groups', 'blk')), parts along dimension 0
- numer: float32 [32, 32, 256], P(('groups', 'blk')), parts along dimension 0
- denom: float32 [32, 32, 256], P(('groups', 'blk')), parts along dimension 0
The draws below stay inside these ranges and needn't reach their ends.
There are 2 independent parts, one for each index of `groups`. The reference program is written for one: setup_inputs(seed, part) draws one part's arguments, and reference() takes and returns one part's arrays. A program takes and returns all parts, laid end to end along the dimension named above; each array names one. Nothing has to cross between parts.
Inputs may be any that keep to these rules, and one draw needn't show every extreme that they name: In the rows of one device no owner is named more than 12 times, a bound that some block reaches.
All inputs are finite; a program needn't handle non-finite values.
Results may differ from the reference program's by a relative error of at most 0.012.
Values may be sent and summed in bfloat16 or wider, within the bound.
A program may use at most 128 MiB of HBM per device.

```python
import math
import jax
import jax.numpy as jnp
import numpy as np
from jax import lax

CYCLES = 32
ANG = 128
BOX = 128
ROTS = 36
SHIFT = 5
MIC_DEV = 6
P_DEV = 128
CLASSES = 16
PARTICLES = 2048
MICS = 96
CAP = 12
N_BLK = 16


def draw_refs(key, part):
    key = jax.random.fold_in(key, 11)
    noise = jnp.clip(jax.random.normal(jax.random.fold_in(key, 1), (CLASSES, CYCLES, 2 * ANG), jnp.float32), -6.0, 6.0)
    spread = jax.random.uniform(jax.random.fold_in(key, 2), (CLASSES, 1, 1), jnp.float32, 0.97, 1.03)
    level = 0.16
    return (noise * spread * level).astype(jnp.bfloat16)


def draw_ctf(key, part):
    key = jax.random.fold_in(key, 23)
    defocus = jax.random.uniform(jax.random.fold_in(key, 1), (MICS, 1, 1), jnp.float32, 4.0, 12.0)
    astig = jax.random.uniform(jax.random.fold_in(key, 2), (MICS, 1, 1), jnp.float32, 0.0, 0.3)
    axis_angle = jax.random.uniform(jax.random.fold_in(key, 3), (MICS, 1, 1), jnp.float32, -jnp.pi, jnp.pi)
    radius = jnp.arange(1, CYCLES + 1, dtype=jnp.float32)[None, :, None] / CYCLES
    azimuth = 2.0 * jnp.pi * jnp.arange(ANG, dtype=jnp.float32)[None, None, :] / ANG
    phase = defocus * radius * radius * (1.0 + astig * jnp.cos(2.0 * (azimuth - axis_angle))) + 0.1
    return (-jnp.sin(phase)).astype(jnp.bfloat16)


def with_ends(values, key, smallest, top_value):
    longest = values.shape.index(max(values.shape))
    spots = []
    for shift in (0, 1):
        where = [jax.random.randint(jax.random.fold_in(key, axis), (), 0, length) for axis, length in enumerate(values.shape)]
        where[longest] = (where[longest] + shift) % values.shape[longest]
        spots.append(tuple(where))
    return values.at[spots[0]].set(smallest).at[spots[1]].set(top_value)


def steps_of(rng, dims, split, least, top_value):
    factor_of = 1.0
    for position, blocks in split:
        steps = jax.random.uniform(jax.random.fold_in(jax.random.fold_in(rng, 6), position), (blocks,), jnp.float32, least / len(split), top_value / len(split))
        factor_of = factor_of * jnp.repeat(jnp.exp(steps), dims[position] // blocks).reshape((-1,) + (1,) * (len(dims) - 1 - position))
    return factor_of


def routed_block(stream_key, own, number, rows, count, top, bound, lean):
    ranking = jax.random.permutation(stream_key, count)
    packed, common = load_shares(count, rows * top, bound, lean, True), load_shares(count, rows * top, bound, lean, False)
    places = jnp.arange(count)

    def named(tallies, rotation):
        used = int((tallies > 0).sum())
        fixed = max(1, used // 4)
        passed = fixed + (places - fixed + rotation * (used - fixed)) % max(1, count - fixed)
        return jnp.zeros((count,), jnp.int32).at[ranking[jnp.where(places < fixed, places, passed)]].set(jnp.asarray(tallies, jnp.int32))

    tallies = jnp.where(number % 4 == 0, named(packed, number // 4), named(common, number - number // 4 - 1))
    mixed = jax.random.permutation(jax.random.fold_in(own, 3), count)
    source_of, sink = mixed[0:count // 2 * 2:2], mixed[1:count // 2 * 2:2]
    margin = jnp.minimum(tallies[source_of] - 1, bound - tallies[sink]) // 2
    margin = jnp.where((source_of == ranking[0]) | (sink == ranking[0]) | (tallies[sink] == 0), 0, jnp.maximum(margin, 0))
    passed = jax.random.randint(jax.random.fold_in(own, 4), (count // 2,), 0, 1 << 20) % (margin + 1)
    tallies = tallies.at[source_of].add(-passed).at[sink].add(passed)
    members = jnp.searchsorted(jnp.cumsum(tallies), jnp.arange(rows * top), side="right").astype(jnp.int32)
    listing = members.reshape(top, rows).T
    listing = listing[jax.random.permutation(jax.random.fold_in(own, 1), rows)]
    rotation = jax.random.randint(jax.random.fold_in(own, 2), (rows, 1), 0, top)
    return jnp.take_along_axis(listing, (jnp.arange(top)[None, :] + rotation) % top, axis=1)


def load_shares(count, total, limit, slope, full):
    weights = [(1 << 20) // math.isqrt(standing ** slope) + 1 for standing in range(1, count + 1)]
    largest = limit if full else min(limit, max(-(-total // count), total * weights[0] // sum(weights)))
    least = 1 if total - largest >= count - 1 else 0
    counts, rest = [largest] + [least] * (count - 1), total - largest - least * (count - 1)
    while rest > 0:
        candidates = [i for i in range(1, count) if counts[i] < largest] or [i for i in range(1, count) if counts[i] < limit]
        whole, left = sum([weights[i] for i in candidates]), rest
        for i in candidates:
            extra = min(limit - counts[i], max(1, left * weights[i] // whole), rest)
            counts[i] = counts[i] + extra
            rest = rest - extra
    return np.array(counts)


def bell_draw(key, shape, deviation, most, cuts=(), held_as=jnp.bfloat16):
    values = deviation * jax.random.normal(key, shape, jnp.float32)
    if cuts:
        values = values * steps_of(key, shape, cuts, -0.22, 0.18)
    return jnp.clip(values, -most, most).astype(held_as)


def setup_inputs(seed: int = 0, part: int = 0) -> dict:
    key_list = jax.random.split(jax.random.key(seed), 8)
    part_keys = jax.random.split(jax.random.fold_in(key_list[7], part), 8)
    particles = bell_draw(part_keys[0], (PARTICLES, CYCLES, 2 * ANG), 1.0, 6.0, ((0, 16),))
    owner_keys = jax.random.split(jax.random.fold_in(part_keys[1], 1), PARTICLES // P_DEV)
    owner_turns = jax.random.permutation(jax.random.fold_in(part_keys[1], 3), PARTICLES // P_DEV)
    owner = jax.vmap(lambda own, number: routed_block(jax.random.fold_in(part_keys[1], 2), own, number, P_DEV, N_BLK, 1, CAP, 2))(owner_keys, owner_turns).reshape((PARTICLES, 1))
    mic_local = with_ends(jax.random.randint(part_keys[2], (PARTICLES,), 0, MIC_DEV), jax.random.fold_in(part_keys[2], 1), 0, MIC_DEV - 1).astype(jnp.int32)
    shifts = with_ends(jax.random.randint(part_keys[3], (PARTICLES, 2), -SHIFT, SHIFT + 1), jax.random.fold_in(part_keys[3], 1), -SHIFT, SHIFT).astype(jnp.int32)
    prior = with_ends(jax.random.randint(part_keys[4], (PARTICLES,), 0, 360 // ROTS), jax.random.fold_in(part_keys[4], 1), 0, (360 // ROTS) - 1).astype(jnp.int32)
    refs = draw_refs(jax.random.fold_in(jax.random.fold_in(key_list[7], part), 71), part)
    ctf = draw_ctf(jax.random.fold_in(jax.random.fold_in(key_list[7], part), 71), part)
    return dict(particles=particles, owner=owner, mic_local=mic_local, shifts=shifts, prior=prior, refs=refs, ctf=ctf)


HIGH = lax.Precision.HIGHEST


def spectral_tables(angles, rotations):
    sample = jnp.arange(angles, dtype=jnp.float32)
    azimuth = 2.0 * jnp.pi * sample / angles
    order = jnp.where(sample < angles // 2, sample, sample - angles)
    phase = azimuth[:, None] * order[None, :]
    cosine = jnp.cos(phase)
    sine = jnp.sin(phase)
    forward = jnp.concatenate([jnp.concatenate([cosine, -sine], 1), jnp.concatenate([sine, cosine], 1)], 0)
    turns = 2.0 * jnp.pi * jnp.arange(rotations, dtype=jnp.float32) / rotations
    spin = order[:, None] * turns[None, :]
    rotate = jnp.concatenate([jnp.cos(spin), jnp.sin(spin)], 0)
    return forward, rotate, azimuth, order


def turn_spectra(spectra, prior_steps, order):
    angles = order.shape[0]
    theta = 2.0 * jnp.pi * prior_steps.astype(jnp.float32) / 360.0
    spin = theta[:, None, None] * order[None, None, :]
    cosine = jnp.cos(spin)
    sine = jnp.sin(spin)
    real_part = spectra[..., :angles]
    imag_part = spectra[..., angles:]
    return jnp.concatenate([real_part * cosine - imag_part * sine, real_part * sine + imag_part * cosine], -1)


def image_spectra(images, ctf_rows, offsets, prior_steps, forward, azimuth, order):
    angles = azimuth.shape[0]
    cycles = images.shape[1]
    values = images.astype(jnp.float32)
    real_part = values[..., :angles]
    imag_part = values[..., angles:]
    radius = jnp.arange(1, cycles + 1, dtype=jnp.float32)
    travel = offsets[:, 0].astype(jnp.float32)[:, None] * jnp.cos(azimuth)[None, :] + offsets[:, 1].astype(jnp.float32)[:, None] * jnp.sin(azimuth)[None, :]
    phase = (-2.0 * jnp.pi / BOX) * radius[None, :, None] * travel[:, None, :]
    cosine = jnp.cos(phase)
    sine = jnp.sin(phase)
    shifted = jnp.concatenate([ctf_rows * (real_part * cosine - imag_part * sine), ctf_rows * (real_part * sine + imag_part * cosine)], -1)
    spectra = jnp.matmul(shifted, forward, precision=HIGH)
    return turn_spectra(spectra, prior_steps, order).astype(jnp.bfloat16)


def power_spectra(ctf_rows, forward):
    angles = ctf_rows.shape[-1]
    return jnp.matmul(ctf_rows * ctf_rows, forward[:angles], precision=HIGH)


def correlation(left, right):
    angles = left.shape[-1] // 2
    left_re = left[..., :angles].astype(jnp.float32)
    left_im = left[..., angles:].astype(jnp.float32)
    right_re = right[..., :angles].astype(jnp.float32)
    right_im = right[..., angles:].astype(jnp.float32)
    form = "ipm,kpm->ikm"
    real_sum = jnp.einsum(form, left_re, right_re, precision=HIGH) + jnp.einsum(form, left_im, right_im, precision=HIGH)
    imag_sum = jnp.einsum(form, left_re, right_im, precision=HIGH) - jnp.einsum(form, left_im, right_re, precision=HIGH)
    return jnp.concatenate([real_sum, imag_sum], -1)


def accumulate(spun, spectra):
    angles = spun.shape[-1] // 2
    spun_re = spun[..., :angles].astype(jnp.float32)
    spun_im = spun[..., angles:].astype(jnp.float32)
    spec_re = spectra[..., :angles].astype(jnp.float32)
    spec_im = spectra[..., angles:].astype(jnp.float32)
    form = "ikm,ipm->kpm"
    real_sum = jnp.einsum(form, spun_re, spec_re, precision=HIGH) - jnp.einsum(form, spun_im, spec_im, precision=HIGH)
    imag_sum = jnp.einsum(form, spun_re, spec_im, precision=HIGH) + jnp.einsum(form, spun_im, spec_re, precision=HIGH)
    return jnp.concatenate([real_sum, imag_sum], -1)


def reference(particles, owner, mic_local, shifts, prior, refs, ctf):
    forward, rotate, azimuth, order = spectral_tables(ANG, ROTS)
    micro = owner[:, 0] * MIC_DEV + mic_local
    ref_values = refs.astype(jnp.float32)
    ref_spectra = jnp.matmul(ref_values, forward, precision=HIGH).astype(jnp.bfloat16)
    ref_power = ref_values[..., :ANG] ** 2 + ref_values[..., ANG:] ** 2
    ref_power_spectra = jnp.matmul(ref_power, forward[:ANG], precision=HIGH).astype(jnp.bfloat16)
    block = math.gcd(PARTICLES, 256)
    number = PARTICLES // block

    def batched(array):
        return array.reshape((number, block) + array.shape[1:])

    def advance(carry, inputs):
        images, micro_rows, offsets, prior_rows = inputs
        ctf_rows = ctf[micro_rows].astype(jnp.float32)
        spectra = image_spectra(images, ctf_rows, offsets, prior_rows, forward, azimuth, order)
        ctf_spectra = turn_spectra(power_spectra(ctf_rows, forward), prior_rows, order).astype(jnp.bfloat16)
        mixed = correlation(spectra, ref_spectra) - 0.5 * correlation(ctf_spectra, ref_power_spectra)
        scores = (jnp.matmul(mixed, rotate, precision=HIGH) / ANG).reshape(block, CLASSES * ROTS)
        peak = jnp.max(scores, axis=1, keepdims=True)
        expo = jnp.exp(scores - peak)
        total = jnp.sum(expo, axis=1, keepdims=True)
        weights = expo / total
        evidence = (peak + jnp.log(total))[:, 0]
        posterior = jnp.sum(weights.reshape(block, CLASSES, ROTS), axis=2)
        spun = jnp.matmul(weights.reshape(block, CLASSES, ROTS), rotate.T, precision=HIGH).astype(jnp.bfloat16)
        terms = jnp.stack([accumulate(spun, spectra), accumulate(spun, ctf_spectra)], 1)
        return carry + terms, (posterior, evidence)

    start_sums = jnp.zeros((CLASSES, 2, CYCLES, 2 * ANG), jnp.float32)
    sums, outputs = lax.scan(advance, start_sums, (batched(particles), batched(micro), batched(shifts), batched(prior)))
    posterior, evidence = outputs
    return posterior.reshape(PARTICLES, CLASSES), evidence.reshape(PARTICLES), sums[:, 0], sums[:, 1]
```

```python
import functools

import jax
import jax.numpy as jnp
import numpy as np
from jax import lax
from jax.experimental import pallas as pl
from jax.experimental.pallas import tpu as pltpu
from jax.sharding import PartitionSpec as P

BOX = 128
ROTS = 36
ROWS = 40
SHIFT = 5
HIGH = lax.Precision.HIGHEST
MESH = pl.DeviceIdType.MESH
F32 = jnp.float32
BF16 = jnp.bfloat16
VMEM = pl.BlockSpec(memory_space=pltpu.VMEM)
SMEM = pl.BlockSpec(memory_space=pltpu.SMEM)
MIB = 1 << 20


def split_table(table):
    high = table.astype(np.float32).astype(BF16)
    low = (table - high.astype(np.float64)).astype(np.float32).astype(BF16)
    return high, low


def tables(angles, cycles):
    sample = np.arange(angles)
    order = np.where(sample < angles // 2, sample, sample - angles)
    phase = 2.0 * np.pi * ((sample[:, None] * order[None, :]) % angles) / angles
    cosine, sine = np.cos(phase), np.sin(phase)
    forward = np.block([[cosine, -sine], [sine, cosine]])
    spin = 2.0 * np.pi * ((order[:, None] * np.arange(ROTS)[None, :]) % ROTS) / ROTS
    rotate = np.zeros((2 * angles, ROWS))
    rotate[:, :ROTS] = np.concatenate([np.cos(spin), np.sin(spin)], 0)
    azimuth = 2.0 * np.pi * sample / angles
    step = np.arange(-SHIFT, SHIFT + 1)[:, None, None] * np.arange(1, cycles + 1)[None, :, None]
    moves = []
    for part in (np.cos(azimuth), np.sin(azimuth)):
        turn = -2.0 * np.pi / BOX * step * part[None, None, :]
        moves.append(np.concatenate([np.cos(turn), np.sin(turn)], -1).astype(np.float32))
    return forward, rotate, moves, order


def neighbours(devices):
    me = lax.axis_index("blk")
    core = lax.rem(me, 2)
    side = lax.rem(me // 2, 2)
    layer = me // 4
    return me, core, side, layer, devices // 4


def greet(partners):
    barrier = pltpu.get_barrier_semaphore()
    for partner in partners:
        pl.semaphore_signal(barrier, inc=1, device_id={"blk": partner}, device_id_type=MESH)
    pl.semaphore_wait(barrier, len(partners))


def gather_kernel(devices, own_ref, all_ref, send_sem, recv_sem):
    me, core, side, layer, layers = neighbours(devices)
    column = side * 2 + core
    across = (1 - side) * 2 + core
    sibling = me + 1 - 2 * core
    beside = me + 2 - 4 * side
    others = [lax.rem(layer + hop, layers) for hop in range(1, layers)]
    greet([other * 4 + column for other in others] + [sibling, beside])
    sent = []

    def send(source, block, target, slot):
        copy = pltpu.make_async_remote_copy(
            src_ref=source,
            dst_ref=all_ref.at[block],
            send_sem=send_sem.at[slot],
            recv_sem=recv_sem.at[block],
            device_id={"blk": target},
            device_id_type=MESH,
        )
        copy.start()
        sent.append(copy)

    def arrive(block):
        pltpu.make_async_remote_copy(
            src_ref=own_ref,
            dst_ref=all_ref.at[block],
            send_sem=send_sem.at[0],
            recv_sem=recv_sem.at[block],
            device_id={"blk": sibling},
            device_id_type=MESH,
        ).wait_recv()

    for hop, other in enumerate(others):
        send(own_ref, me, other * 4 + column, hop)
    send(own_ref, me, beside, layers)
    send(own_ref, me, sibling, 2 * layers)
    all_ref[me] = own_ref[...]
    far = me + 2 - 4 * side
    for hop in range(layers):
        if hop > 0:
            block = others[hop - 1] * 4 + column
            arrive(block)
            send(all_ref.at[block], block, beside, layers + hop)
            send(all_ref.at[block], block, sibling, 2 * layers + hop)
        far = (layer if hop == 0 else others[hop - 1]) * 4 + across
        arrive(far)
        send(all_ref.at[far], far, sibling, 3 * layers + hop)
    for hop in range(layers):
        place = (layer if hop == 0 else others[hop - 1]) * 4
        arrive(place + side * 2 + 1 - core)
        arrive(place + (1 - side) * 2 + 1 - core)
    for copy in sent:
        copy.wait_send()


def gather_blocks(own, devices):
    return pl.pallas_call(
        functools.partial(gather_kernel, devices),
        out_shape=jax.ShapeDtypeStruct((devices,) + own.shape, own.dtype),
        in_specs=[VMEM],
        out_specs=VMEM,
        scratch_shapes=[
            pltpu.SemaphoreType.DMA((devices,)),
            pltpu.SemaphoreType.DMA((devices,)),
        ],
        compiler_params=pltpu.CompilerParams(
            collective_id=0, has_side_effects=True, vmem_limit_bytes=48 * MIB
        ),
    )(own)


def reduce_kernel(devices, local, part_ref, numer_ref, denom_ref, *scratch):
    near, side_in, layer_in, side_out, layer_out, send_sem, near_sem, side_sem, layer_sem = scratch
    me, core, side, layer, layers = neighbours(devices)
    column = side * 2 + core
    sibling = me + 1 - 2 * core
    beside = me + 2 - 4 * side
    depth = part_ref.shape[0] // devices
    others = [lax.rem(layer + hop, layers) for hop in range(1, layers)]
    hops = list(range(1, layers)) + [0]
    greet([other * 4 + column for other in others] + [sibling, beside])

    def rows(block):
        return pl.ds(pl.multiple_of(block * depth, depth), depth)

    def target(hop):
        return layer if hop == 0 else others[hop - 1]

    def copy_to(source, sink, number, sem, device):
        return pltpu.make_async_remote_copy(
            src_ref=source,
            dst_ref=sink,
            send_sem=send_sem.at[number],
            recv_sem=sem,
            device_id={"blk": device},
            device_id_type=MESH,
        )

    first, second, third = {}, {}, {}
    for hop in hops:
        for flip in (1, 0):
            place = jnp.where(side == 1, 1 - flip, flip) if flip else side
            block = target(hop) * 4 + place * 2 + 1 - core
            slot = 2 * hop + flip
            first[slot] = copy_to(
                part_ref.at[rows(block)], near.at[slot], slot, near_sem.at[slot], sibling
            )
            first[slot].start()
    for hop in hops:
        first[2 * hop + 1].wait_recv()
        block = target(hop) * 4 + (1 - side) * 2 + core
        side_out[hop] = part_ref[rows(block), :] + near[2 * hop + 1]
        second[hop] = copy_to(
            side_out.at[hop], side_in.at[hop], 2 * layers + hop, side_sem.at[hop], beside
        )
        second[hop].start()
    for hop in hops:
        first[2 * hop].wait_recv()
        second[hop].wait_recv()
        block = target(hop) * 4 + column
        layer_out[hop] = part_ref[rows(block), :] + near[2 * hop] + side_in[hop]
        if hop:
            third[hop] = copy_to(
                layer_out.at[hop],
                layer_in.at[hop],
                3 * layers + hop,
                layer_sem.at[hop],
                target(hop) * 4 + column,
            )
            third[hop].start()
    total = layer_out[0]
    for hop in range(1, layers):
        third[hop].wait_recv()
        total = total + layer_in[hop]
    cycles, angles = numer_ref.shape[1], numer_ref.shape[2] // 2
    for item in range(local):
        turned = total[item * angles : (item + 1) * angles].T
        numer_ref[item, :, :angles] = turned[:cycles]
        denom_ref[item, :, :angles] = turned[cycles : 2 * cycles]
        numer_ref[item, :, angles:] = turned[2 * cycles : 3 * cycles]
        denom_ref[item, :, angles:] = turned[3 * cycles :]
    for copies in (first, second, third):
        for copy in copies.values():
            copy.wait_send()


def reduce_blocks(parts, devices, local, cycles, angles):
    layers = devices // 4
    depth = local * angles
    lanes = parts.shape[1]
    shape = jax.ShapeDtypeStruct((local, cycles, 2 * angles), F32)
    return pl.pallas_call(
        functools.partial(reduce_kernel, devices, local),
        out_shape=(shape, shape),
        in_specs=[VMEM],
        out_specs=(VMEM, VMEM),
        scratch_shapes=[
            pltpu.VMEM((2 * layers, depth, lanes), F32),
            pltpu.VMEM((layers, depth, lanes), F32),
            pltpu.VMEM((layers, depth, lanes), F32),
            pltpu.VMEM((layers, depth, lanes), F32),
            pltpu.VMEM((layers, depth, lanes), F32),
            pltpu.SemaphoreType.DMA((4 * layers,)),
            pltpu.SemaphoreType.DMA((2 * layers,)),
            pltpu.SemaphoreType.DMA((layers,)),
            pltpu.SemaphoreType.DMA((layers,)),
        ],
        compiler_params=pltpu.CompilerParams(
            collective_id=1, has_side_effects=True, vmem_limit_bytes=48 * MIB
        ),
    )(parts)


def halves(value):
    high = value.astype(BF16)
    return high, (value - high.astype(F32)).astype(BF16)


def dot(left, right):
    return jnp.dot(left, right, preferred_element_type=F32)


def dot_nt(left, right):
    return lax.dot_general(left, right, (((1,), (1,)), ((), ())), preferred_element_type=F32)


def score_kernel(sizes, index_ref, images_ref, all_ref, move_x_ref, move_y_ref, turn_ref,
                 forward_ref, rotate_ref, spread_ref, post_ref, evid_ref, parts_ref,
                 work, spec, refs):
    count, cycles, angles, classes, mics = sizes
    depth = 4 * cycles
    plane = cycles * count

    def shift_one(i):
        own, mic = index_ref[0, i], index_ref[1, i]
        move_x, move_y = move_x_ref[index_ref[2, i] + SHIFT], move_y_ref[index_ref[3, i] + SHIFT]
        row = pl.multiple_of(mic * cycles, cycles)
        transfer = all_ref[own, pl.ds(row, cycles), :].astype(F32)
        image = images_ref[i].astype(F32)
        x_re, x_im = move_x[:, :angles], move_x[:, angles:]
        y_re, y_im = move_y[:, :angles], move_y[:, angles:]
        re = x_re * y_re - x_im * y_im
        im = x_re * y_im + x_im * y_re
        a_re, a_im = image[:, :angles], image[:, angles:]
        work[pl.ds(i, cycles, stride=count), :] = transfer * (a_re * re - a_im * im)
        work[pl.ds(plane + i, cycles, stride=count), :] = transfer * (a_re * im + a_im * re)
        work[pl.ds(2 * plane + i, cycles, stride=count), :] = transfer * transfer

    @pl.loop(0, count // 4)
    def _(group):
        for u in range(4):
            shift_one(group * 4 + u)

    def place_ref(k):
        base = mics * cycles
        half = all_ref[k // sizes_local, pl.ds(base + (k % sizes_local) * angles, angles), :]
        value = half.astype(F32)
        lane = lax.broadcasted_iota(jnp.int32, value.shape, 1)
        swapped = pltpu.roll(value, depth // 2, 1)
        swapped = jnp.where(lane < depth // 2, swapped, -swapped)
        refs[pl.ds(k, angles, stride=2 * classes), :] = value
        refs[pl.ds(classes + k, angles, stride=2 * classes), :] = swapped

    sizes_local = classes // all_ref.shape[0]

    @pl.loop(0, classes // 2)
    def _(group):
        for u in range(2):
            place_ref(group * 2 + u)

    turn_re, turn_im = turn_ref[:angles], turn_ref[angles:]

    def put(values, start):
        re, im = values[:angles], values[angles:]
        spec[pl.ds(start, angles, stride=depth), :] = re * turn_re - im * turn_im
        spec[pl.ds(2 * cycles + start, angles, stride=depth), :] = re * turn_im + im * turn_re

    def transform(p):
        rows = pl.ds(pl.multiple_of(p * count, count), count)
        re = work[rows, :]
        im = work[pl.ds(pl.multiple_of(plane + p * count, count), count), :]
        power = work[pl.ds(pl.multiple_of(2 * plane + p * count, count), count), :]
        high, low = halves(jnp.concatenate([re, im], 1))
        f_high, f_low = forward_ref[0], forward_ref[1]
        values = dot_nt(f_high, high) + dot_nt(f_low, high) + dot_nt(f_high, low)
        put(values, p)
        high, low = halves(power)
        f_high, f_low = f_high[:, :angles], f_low[:, :angles]
        values = dot_nt(f_high, high) + dot_nt(f_low, high) + dot_nt(f_high, low)
        put(values, cycles + p)

    @pl.loop(0, cycles // 2)
    def _(group):
        for u in range(2):
            transform(group * 2 + u)

    def correlate(m):
        held = spec[pl.ds(pl.multiple_of(m * depth, depth), depth), :].astype(BF16)
        rows = pl.ds(pl.multiple_of(m * 2 * classes, 2 * classes), 2 * classes)
        parts_ref[pl.ds(m, 2 * classes, stride=angles), :] = dot(refs[rows, :].astype(BF16), held)

    @pl.loop(0, angles // 8)
    def _(group):
        for u in range(8):
            correlate(group * 8 + u)

    scale = 1.0 / angles
    valid = lax.broadcasted_iota(jnp.int32, (ROWS, count), 0) < ROTS

    def score(k, peak):
        re = parts_ref[pl.ds(pl.multiple_of(k * angles, angles), angles), :]
        im = parts_ref[pl.ds(pl.multiple_of((classes + k) * angles, angles), angles), :]
        high, low = halves(jnp.concatenate([re, im], 0))
        r_high, r_low = rotate_ref[0], rotate_ref[1]
        value = (dot(r_high, high) + dot(r_low, high) + dot(r_high, low)) * scale
        value = jnp.where(valid, value, -jnp.inf)
        work[pl.ds(pl.multiple_of(k * ROWS, 8), ROWS), :] = value
        return jnp.maximum(peak, value)

    def score_two(group, peak):
        return score(group * 2 + 1, score(group * 2, peak))

    peak = lax.fori_loop(0, classes // 2, score_two, jnp.full((ROWS, count), -jnp.inf, F32))
    peak = jnp.max(peak, axis=0, keepdims=True)

    def expo(k, total):
        rows = pl.ds(pl.multiple_of(k * ROWS, 8), ROWS)
        value = jnp.exp(work[rows, :] - peak)
        work[rows, :] = value
        return total + value

    total = lax.fori_loop(0, classes, expo, jnp.zeros((ROWS, count), F32))
    total = jnp.sum(total, axis=0, keepdims=True)
    evid_ref[...] = peak + jnp.log(total)
    share = 1.0 / total

    def unrotate(k):
        weights = work[pl.ds(pl.multiple_of(k * ROWS, 8), ROWS), :] * share
        post_ref[pl.ds(k, 1), :] = jnp.sum(weights, axis=0, keepdims=True)
        high, low = halves(weights)
        stacked = jnp.concatenate(
            [high.astype(F32), high.astype(F32), low.astype(F32), jnp.zeros((8, count), F32)], 0
        ).astype(BF16)
        value = dot(spread_ref[...], stacked)
        refs[pl.ds(k, angles, stride=2 * classes), :] = value[:angles]
        refs[pl.ds(classes + k, angles, stride=2 * classes), :] = value[angles:]

    @pl.loop(0, classes // 2)
    def _(group):
        for u in range(2):
            unrotate(group * 2 + u)

    def gather_up(m):
        held = spec[pl.ds(pl.multiple_of(m * depth, depth), depth), :]
        other = jnp.concatenate([-held[depth // 2 :], held[: depth // 2]], 0)
        right = jnp.concatenate([held, other], 1).astype(BF16)
        rows = pl.ds(pl.multiple_of(m * 2 * classes, 2 * classes), 2 * classes)
        spun = refs[rows, :]
        left = jnp.concatenate([spun[:classes], spun[classes:]], 1).astype(BF16)
        parts_ref[pl.ds(m, classes, stride=angles), :] = dot_nt(left, right)

    @pl.loop(0, angles // 8)
    def _(group):
        for u in range(8):
            gather_up(group * 8 + u)


def per_device(particles, owner, mic_local, shifts, prior, refs, ctf):
    devices = lax.axis_size("blk")
    count, cycles, angles = particles.shape[0], particles.shape[1], particles.shape[2] // 2
    local = refs.shape[0]
    classes = local * devices
    mics = ctf.shape[0]
    forward, rotate, moves, order = tables(angles, cycles)

    values = refs.astype(F32)
    table = jnp.asarray(forward.astype(np.float32))
    spectra = jnp.matmul(values, table, precision=HIGH).astype(BF16)
    power = values[..., :angles] ** 2 + values[..., angles:] ** 2
    power_spectra = jnp.matmul(power, table[:angles], precision=HIGH).astype(BF16)
    both = jnp.stack([spectra, -0.5 * power_spectra], 1).reshape(local, 2, cycles, 2, angles)
    both = both.transpose(0, 4, 3, 1, 2).reshape(local * angles, 4 * cycles)
    own = jnp.concatenate([ctf.reshape(mics * cycles, angles), both.astype(BF16)], 0)
    everything = gather_blocks(own, devices)

    index = jnp.stack([owner[:, 0], mic_local, shifts[:, 0], shifts[:, 1]])
    theta = 2.0 * jnp.pi * prior.astype(F32) / 360.0
    spin = jnp.asarray(order.astype(np.float32))[:, None] * theta[None, :]
    turn = jnp.concatenate([jnp.cos(spin), jnp.sin(spin)], 0)
    forward_t = jnp.asarray(np.stack(split_table(forward.T)))
    rotate_high, rotate_low = split_table(rotate)
    rotate_t = jnp.asarray(np.stack([rotate_high.T, rotate_low.T]))
    spread = jnp.asarray(
        np.concatenate(
            [rotate_high, rotate_low, rotate_high, np.zeros((2 * angles, 8), BF16)], 1
        )
    )
    post, evidence, parts = pl.pallas_call(
        functools.partial(score_kernel, (count, cycles, angles, classes, mics)),
        out_shape=(
            jax.ShapeDtypeStruct((classes, count), F32),
            jax.ShapeDtypeStruct((1, count), F32),
            jax.ShapeDtypeStruct((2 * classes * angles, 4 * cycles), F32),
        ),
        in_specs=[SMEM] + [VMEM] * 8,
        out_specs=(VMEM, VMEM, VMEM),
        scratch_shapes=[
            pltpu.VMEM((3 * cycles * count, angles), F32),
            pltpu.VMEM((angles * 4 * cycles, count), F32),
            pltpu.VMEM((2 * classes * angles, count), F32),
        ],
        compiler_params=pltpu.CompilerParams(vmem_limit_bytes=63 * MIB),
    )(index, particles, everything, jnp.asarray(moves[0]), jnp.asarray(moves[1]), turn,
      forward_t, rotate_t, spread)
    numer, denom = reduce_blocks(parts[: classes * angles], devices, local, cycles, angles)
    return post.T, evidence[0], numer, denom


def solution(mesh):
    in_specs = (
        P(("groups", "blk"), None, None),
        P(("groups", "blk"), None),
        P(("groups", "blk")),
        P(("groups", "blk"), None),
        P(("groups", "blk")),
        P(("groups", "blk"), None, None),
        P(("groups", "blk"), None, None),
    )
    out_specs = (
        P(("groups", "blk"), None),
        P(("groups", "blk")),
        P(("groups", "blk"), None, None),
        P(("groups", "blk"), None, None),
    )
    return jax.shard_map(
        per_device, mesh=mesh, in_specs=in_specs, out_specs=out_specs, check_vma=False
    )
```

```python
import functools

import jax
import jax.numpy as jnp
import numpy as np
from jax import lax
from jax.experimental import pallas as pl
from jax.experimental.pallas import tpu as pltpu
from jax.sharding import PartitionSpec as P

BOX = 128
ROTS = 36
ROWS = 40
SHIFT = 5
HIGH = lax.Precision.HIGHEST
MESH = pl.DeviceIdType.MESH
F32 = jnp.float32
BF16 = jnp.bfloat16
VMEM = pl.BlockSpec(memory_space=pltpu.VMEM)
SMEM = pl.BlockSpec(memory_space=pltpu.SMEM)
MIB = 1 << 20
PAD = 8
CHUNKS = 4


def split_table(table):
    high = table.astype(np.float32).astype(BF16)
    low = (table - high.astype(np.float64)).astype(np.float32).astype(BF16)
    return high, low


def tables(angles, cycles):
    sample = np.arange(angles)
    order = np.where(sample < angles // 2, sample, sample - angles)
    phase = 2.0 * np.pi * ((sample[:, None] * order[None, :]) % angles) / angles
    cosine, sine = np.cos(phase), np.sin(phase)
    forward = np.block([[cosine, -sine], [sine, cosine]])
    spin = 2.0 * np.pi * ((order[:, None] * np.arange(ROTS)[None, :]) % ROTS) / ROTS
    rotate = np.zeros((2 * angles, ROWS))
    rotate[:, :ROTS] = np.concatenate([np.cos(spin), np.sin(spin)], 0)
    azimuth = 2.0 * np.pi * sample / angles
    step = np.arange(-SHIFT, SHIFT + 1)[:, None, None] * np.arange(1, cycles + 1)[None, :, None]
    moves = []
    for part in (np.cos(azimuth), np.sin(azimuth)):
        turn = -2.0 * np.pi / BOX * step * part[None, None, :]
        moves.append(np.concatenate([np.cos(turn), np.sin(turn)], -1))
    return forward, rotate, moves, order


def neighbours(devices):
    me = lax.axis_index("blk")
    core = lax.rem(me, 2)
    side = lax.rem(me // 2, 2)
    layer = me // 4
    return me, core, side, layer, devices // 4


def greet(partners):
    barrier = pltpu.get_barrier_semaphore()
    for partner in partners:
        pl.semaphore_signal(barrier, inc=1, device_id={"blk": partner}, device_id_type=MESH)
    pl.semaphore_wait(barrier, len(partners))


def gather_kernel(devices, own_ref, all_ref, send_sem, recv_sem):
    me, core, side, layer, layers = neighbours(devices)
    column = side * 2 + core
    across = (1 - side) * 2 + core
    sibling = me + 1 - 2 * core
    beside = me + 2 - 4 * side
    others = [lax.rem(layer + hop, layers) for hop in range(1, layers)]
    greet([other * 4 + column for other in others] + [sibling, beside])
    sent = []

    def send(source, block, target, slot):
        copy = pltpu.make_async_remote_copy(
            src_ref=source,
            dst_ref=all_ref.at[block],
            send_sem=send_sem.at[slot],
            recv_sem=recv_sem.at[block],
            device_id={"blk": target},
            device_id_type=MESH,
        )
        copy.start()
        sent.append(copy)

    def arrive(block):
        pltpu.make_async_remote_copy(
            src_ref=own_ref,
            dst_ref=all_ref.at[block],
            send_sem=send_sem.at[0],
            recv_sem=recv_sem.at[block],
            device_id={"blk": sibling},
            device_id_type=MESH,
        ).wait_recv()

    for hop, other in enumerate(others):
        send(own_ref, me, other * 4 + column, hop)
    send(own_ref, me, beside, layers)
    send(own_ref, me, sibling, 2 * layers)
    all_ref[me] = own_ref[...]
    far = me + 2 - 4 * side
    for hop in range(layers):
        if hop > 0:
            block = others[hop - 1] * 4 + column
            arrive(block)
            send(all_ref.at[block], block, beside, layers + hop)
            send(all_ref.at[block], block, sibling, 2 * layers + hop)
        far = (layer if hop == 0 else others[hop - 1]) * 4 + across
        arrive(far)
        send(all_ref.at[far], far, sibling, 3 * layers + hop)
    for hop in range(layers):
        place = (layer if hop == 0 else others[hop - 1]) * 4
        arrive(place + side * 2 + 1 - core)
        arrive(place + (1 - side) * 2 + 1 - core)
    for copy in sent:
        copy.wait_send()


def gather_blocks(own, devices):
    return pl.pallas_call(
        functools.partial(gather_kernel, devices),
        out_shape=jax.ShapeDtypeStruct((devices,) + own.shape, own.dtype),
        in_specs=[VMEM],
        out_specs=VMEM,
        scratch_shapes=[
            pltpu.SemaphoreType.DMA((devices,)),
            pltpu.SemaphoreType.DMA((devices,)),
        ],
        compiler_params=pltpu.CompilerParams(
            collective_id=0, has_side_effects=True, vmem_limit_bytes=48 * MIB
        ),
    )(own)


def reduce_kernel(devices, local, part_ref, numer_ref, denom_ref, *scratch):
    near, side_in, layer_in, side_out, layer_out, send_sem, near_sem, side_sem, layer_sem = scratch
    me, core, side, layer, layers = neighbours(devices)
    column = side * 2 + core
    sibling = me + 1 - 2 * core
    beside = me + 2 - 4 * side
    depth = part_ref.shape[0] // devices
    others = [lax.rem(layer + hop, layers) for hop in range(1, layers)]
    hops = list(range(1, layers)) + [0]
    greet([other * 4 + column for other in others] + [sibling, beside])

    def rows(block):
        return pl.ds(pl.multiple_of(block * depth, depth), depth)

    def target(hop):
        return layer if hop == 0 else others[hop - 1]

    def copy_to(source, sink, number, sem, device):
        return pltpu.make_async_remote_copy(
            src_ref=source,
            dst_ref=sink,
            send_sem=send_sem.at[number],
            recv_sem=sem,
            device_id={"blk": device},
            device_id_type=MESH,
        )

    first, second, third = {}, {}, {}
    for hop in hops:
        for flip in (1, 0):
            place = jnp.where(side == 1, 1 - flip, flip) if flip else side
            block = target(hop) * 4 + place * 2 + 1 - core
            slot = 2 * hop + flip
            first[slot] = copy_to(
                part_ref.at[rows(block)], near.at[slot], slot, near_sem.at[slot], sibling
            )
            first[slot].start()
    for hop in hops:
        first[2 * hop + 1].wait_recv()
        block = target(hop) * 4 + (1 - side) * 2 + core
        side_out[hop] = part_ref[rows(block), :] + near[2 * hop + 1]
        second[hop] = copy_to(
            side_out.at[hop], side_in.at[hop], 2 * layers + hop, side_sem.at[hop], beside
        )
        second[hop].start()
    for hop in hops:
        first[2 * hop].wait_recv()
        second[hop].wait_recv()
        block = target(hop) * 4 + column
        layer_out[hop] = part_ref[rows(block), :] + near[2 * hop] + side_in[hop]
        if hop:
            third[hop] = copy_to(
                layer_out.at[hop],
                layer_in.at[hop],
                3 * layers + hop,
                layer_sem.at[hop],
                target(hop) * 4 + column,
            )
            third[hop].start()
    total = layer_out[0]
    for hop in range(1, layers):
        third[hop].wait_recv()
        total = total + layer_in[hop]
    cycles, angles = numer_ref.shape[1], numer_ref.shape[2] // 2
    for item in range(local):
        turned = total[item * angles : (item + 1) * angles].T
        numer_ref[item, :, :angles] = turned[:cycles]
        denom_ref[item, :, :angles] = turned[cycles : 2 * cycles]
        numer_ref[item, :, angles:] = turned[2 * cycles : 3 * cycles]
        denom_ref[item, :, angles:] = turned[3 * cycles :]
    for copies in (first, second, third):
        for copy in copies.values():
            copy.wait_send()


def reduce_blocks(parts, devices, local, cycles, angles):
    layers = devices // 4
    depth = local * angles
    lanes = parts.shape[1]
    shape = jax.ShapeDtypeStruct((local, cycles, 2 * angles), F32)
    return pl.pallas_call(
        functools.partial(reduce_kernel, devices, local),
        out_shape=(shape, shape),
        in_specs=[VMEM],
        out_specs=(VMEM, VMEM),
        scratch_shapes=[
            pltpu.VMEM((2 * layers, depth, lanes), F32),
            pltpu.VMEM((layers, depth, lanes), F32),
            pltpu.VMEM((layers, depth, lanes), F32),
            pltpu.VMEM((layers, depth, lanes), F32),
            pltpu.VMEM((layers, depth, lanes), F32),
            pltpu.SemaphoreType.DMA((4 * layers,)),
            pltpu.SemaphoreType.DMA((2 * layers,)),
            pltpu.SemaphoreType.DMA((layers,)),
            pltpu.SemaphoreType.DMA((layers,)),
        ],
        compiler_params=pltpu.CompilerParams(
            collective_id=1, has_side_effects=True, vmem_limit_bytes=48 * MIB
        ),
    )(parts)


def halves(value):
    high = value.astype(BF16)
    return high, (value - high.astype(F32)).astype(BF16)


def dot(left, right):
    return jnp.dot(left, right, preferred_element_type=F32)


def dot_nt(left, right):
    return lax.dot_general(left, right, (((1,), (1,)), ((), ())), preferred_element_type=F32)


def score_kernel(sizes, index_ref, images_ref, all_ref, move_x_ref, move_y_ref, turn_ref,
                 forward_ref, rotate_ref, spread_ref, post_ref, evid_ref, parts_ref,
                 work, spec, refs):
    count, cycles, angles, classes, mics = sizes
    depth = 4 * cycles
    plane = cycles * count

    def shift_one(i):
        own, mic = index_ref[0, i], index_ref[1, i]
        move_x, move_y = move_x_ref[index_ref[2, i] + SHIFT], move_y_ref[index_ref[3, i] + SHIFT]
        row = pl.multiple_of(mic * cycles, cycles)
        transfer = all_ref[own, pl.ds(row, cycles), :].astype(F32)
        image = images_ref[i].astype(F32)
        x_re, x_im = move_x[:, :angles], move_x[:, angles:]
        y_re, y_im = move_y[:, :angles], move_y[:, angles:]
        re = x_re * y_re - x_im * y_im
        im = x_re * y_im + x_im * y_re
        a_re, a_im = image[:, :angles], image[:, angles:]
        work[pl.ds(i, cycles, stride=count), :] = transfer * (a_re * re - a_im * im)
        work[pl.ds(plane + i, cycles, stride=count), :] = transfer * (a_re * im + a_im * re)
        work[pl.ds(2 * plane + i, cycles, stride=count), :] = transfer * transfer

    @pl.loop(0, count // 4)
    def _(group):
        for u in range(4):
            shift_one(group * 4 + u)

    def place_ref(k):
        base = mics * cycles
        half = all_ref[k // sizes_local, pl.ds(base + (k % sizes_local) * angles, angles), :]
        value = half.astype(F32)
        lane = lax.broadcasted_iota(jnp.int32, value.shape, 1)
        swapped = pltpu.roll(value, depth // 2, 1)
        swapped = jnp.where(lane < depth // 2, swapped, -swapped)
        refs[pl.ds(k, angles, stride=2 * classes), :] = value
        refs[pl.ds(classes + k, angles, stride=2 * classes), :] = swapped

    sizes_local = classes // all_ref.shape[0]

    @pl.loop(0, classes // 2)
    def _(group):
        for u in range(2):
            place_ref(group * 2 + u)

    turn_re, turn_im = turn_ref[:angles], turn_ref[angles:]

    def put(values, start):
        re, im = values[:angles], values[angles:]
        spec[pl.ds(start, angles, stride=depth), :] = re * turn_re - im * turn_im
        spec[pl.ds(2 * cycles + start, angles, stride=depth), :] = re * turn_im + im * turn_re

    def transform(p):
        rows = pl.ds(pl.multiple_of(p * count, count), count)
        re = work[rows, :]
        im = work[pl.ds(pl.multiple_of(plane + p * count, count), count), :]
        power = work[pl.ds(pl.multiple_of(2 * plane + p * count, count), count), :]
        high, low = halves(jnp.concatenate([re, im], 1))
        f_high, f_low = forward_ref[0], forward_ref[1]
        values = dot_nt(f_high, high) + dot_nt(f_low, high) + dot_nt(f_high, low)
        put(values, p)
        high, low = halves(power)
        f_high, f_low = f_high[:, :angles], f_low[:, :angles]
        values = dot_nt(f_high, high) + dot_nt(f_low, high) + dot_nt(f_high, low)
        put(values, cycles + p)

    @pl.loop(0, cycles // 2)
    def _(group):
        for u in range(2):
            transform(group * 2 + u)

    def correlate(m):
        held = spec[pl.ds(pl.multiple_of(m * depth, depth), depth), :].astype(BF16)
        rows = pl.ds(pl.multiple_of(m * 2 * classes, 2 * classes), 2 * classes)
        parts_ref[pl.ds(m, 2 * classes, stride=angles), :] = dot(refs[rows, :].astype(BF16), held)

    @pl.loop(0, angles // 8)
    def _(group):
        for u in range(8):
            correlate(group * 8 + u)

    scale = 1.0 / angles
    valid = lax.broadcasted_iota(jnp.int32, (ROWS, count), 0) < ROTS

    def score(k, peak):
        re = parts_ref[pl.ds(pl.multiple_of(k * angles, angles), angles), :]
        im = parts_ref[pl.ds(pl.multiple_of((classes + k) * angles, angles), angles), :]
        high, low = halves(jnp.concatenate([re, im], 0))
        r_high, r_low = rotate_ref[0], rotate_ref[1]
        value = (dot(r_high, high) + dot(r_low, high) + dot(r_high, low)) * scale
        value = jnp.where(valid, value, -jnp.inf)
        work[pl.ds(pl.multiple_of(k * ROWS, 8), ROWS), :] = value
        return jnp.maximum(peak, value)

    def score_two(group, peak):
        return score(group * 2 + 1, score(group * 2, peak))

    peak = lax.fori_loop(0, classes // 2, score_two, jnp.full((ROWS, count), -jnp.inf, F32))
    peak = jnp.max(peak, axis=0, keepdims=True)

    def expo(k, total):
        rows = pl.ds(pl.multiple_of(k * ROWS, 8), ROWS)
        value = jnp.exp(work[rows, :] - peak)
        work[rows, :] = value
        return total + value

    total = lax.fori_loop(0, classes, expo, jnp.zeros((ROWS, count), F32))
    total = jnp.sum(total, axis=0, keepdims=True)
    evid_ref[...] = peak + jnp.log(total)
    share = 1.0 / total

    def unrotate(k):
        weights = work[pl.ds(pl.multiple_of(k * ROWS, 8), ROWS), :] * share
        post_ref[pl.ds(k, 1), :] = jnp.sum(weights, axis=0, keepdims=True)
        high, low = halves(weights)
        stacked = jnp.concatenate(
            [high.astype(F32), high.astype(F32), low.astype(F32), jnp.zeros((8, count), F32)], 0
        ).astype(BF16)
        value = dot(spread_ref[...], stacked)
        refs[pl.ds(k, angles, stride=2 * classes), :] = value[:angles]
        refs[pl.ds(classes + k, angles, stride=2 * classes), :] = value[angles:]

    @pl.loop(0, classes // 2)
    def _(group):
        for u in range(2):
            unrotate(group * 2 + u)

    def gather_up(m):
        held = spec[pl.ds(pl.multiple_of(m * depth, depth), depth), :]
        other = jnp.concatenate([-held[depth // 2 :], held[: depth // 2]], 0)
        right = jnp.concatenate([held, other], 1).astype(BF16)
        rows = pl.ds(pl.multiple_of(m * 2 * classes, 2 * classes), 2 * classes)
        spun = refs[rows, :]
        left = jnp.concatenate([spun[:classes], spun[classes:]], 1).astype(BF16)
        parts_ref[pl.ds(m, classes, stride=angles), :] = dot_nt(left, right)

    @pl.loop(0, angles // 8)
    def _(group):
        for u in range(8):
            gather_up(group * 8 + u)


def fused_kernel(sizes, owner_ref, mic_ref, shift_ref, images_ref, ctf_ref, own_values_ref,
                 prior_ref, moves_ref, turns_ref, forward_ref, power_ref,
                 rotate_ref, spread_ref, post_ref, evid_ref, numer_ref, denom_ref,
                 all_ctf, all_refs, own_refs, work, table, phase, spec, refs, mixed, parts,
                 near, side_out, side_in, layer_out, layer_in,
                 ctf_send, ctf_recv, refs_send, refs_recv, near_sems, side_sems, layer_sems):
    devices, count, cycles, angles = sizes
    classes = devices
    depth = 4 * cycles
    lane_rows, deep, pairs, tall = count + PAD, depth + PAD, 2 * classes + PAD, angles + PAD
    plane = cycles * lane_rows
    chunk = angles // CHUNKS
    wide = chunk + PAD

    me, core, side, layer, layers = neighbours(devices)
    column = side * 2 + core
    sibling = me + 1 - 2 * core
    beside = me + 2 - 4 * side
    others = [lax.rem(layer + hop, layers) for hop in range(1, layers)]
    places = [layer] + others
    greet([other * 4 + column for other in others] + [sibling, beside])
    waiting = []

    def push(source, sink, send_sem, recv_sem, device):
        copy = pltpu.make_async_remote_copy(
            src_ref=source,
            dst_ref=sink,
            send_sem=send_sem,
            recv_sem=recv_sem,
            device_id={"blk": device},
            device_id_type=MESH,
        )
        copy.start()
        waiting.append(copy)
        return copy

    def spreader(own, everything, sends, recvs):
        def send(source, block, device, slot):
            push(source, everything.at[block], sends.at[slot], recvs.at[block], device)

        def arrive(block):
            pltpu.make_async_remote_copy(
                src_ref=own,
                dst_ref=everything.at[block],
                send_sem=sends.at[0],
                recv_sem=recvs.at[block],
                device_id={"blk": sibling},
                device_id_type=MESH,
            ).wait_recv()

        def begin():
            for hop, other in enumerate(others):
                send(own, me, other * 4 + column, hop)
            send(own, me, beside, layers)
            send(own, me, sibling, 2 * layers)

        def along(hop):
            block = places[hop] * 4 + column
            arrive(block)
            send(everything.at[block], block, beside, layers + hop)
            send(everything.at[block], block, sibling, 2 * layers + hop)

        def over(hop):
            block = places[hop] * 4 + (1 - side) * 2 + core
            arrive(block)
            send(everything.at[block], block, sibling, 3 * layers + hop)

        def finish():
            for place in places:
                arrive(place * 4 + side * 2 + 1 - core)
                arrive(place * 4 + (1 - side) * 2 + 1 - core)

        return begin, along, over, finish

    ctf_begin, ctf_along, ctf_over, ctf_finish = spreader(ctf_ref, all_ctf, ctf_send, ctf_recv)
    refs_begin, refs_along, refs_over, refs_finish = spreader(
        own_refs, all_refs, refs_send, refs_recv
    )

    ctf_begin()
    all_ctf[me] = ctf_ref[...]
    f_high, f_low = forward_ref[0], forward_ref[1]
    values = own_values_ref[0].astype(F32)
    v_re, v_im = values[:, :angles], values[:, angles:]
    halved = -0.5 * (v_re * v_re + v_im * v_im)
    none = jnp.zeros_like(halved)
    stacked = jnp.concatenate(
        [
            values,
            jnp.concatenate([halved, none], 1),
            jnp.concatenate([v_im, -v_re], 1),
            jnp.concatenate([none, -halved], 1),
        ],
        0,
    )
    high, low = halves(stacked)
    top, bottom = f_high[:angles], f_low[:angles]
    own_block = (dot_nt(top, high) + dot_nt(bottom, high) + dot_nt(top, low)).astype(BF16)
    own_refs[...] = own_block
    all_refs[me] = own_block
    refs_begin()

    def spread_image(i):
        image = images_ref[i].astype(F32)
        work[pl.ds(i, cycles, stride=lane_rows), :] = image[:, :angles]
        work[pl.ds(plane + i, cycles, stride=lane_rows), :] = image[:, angles:]

    def picks(rows, line):
        return (lax.broadcasted_iota(jnp.int32, (rows, count), 0) == line).astype(F32)

    step_x, step_y = picks(16, shift_ref[0:1] + SHIFT), picks(16, shift_ref[1:2] + SHIFT)
    blank = jnp.zeros((32, count), F32)
    moved = jnp.concatenate([step_x] * 3 + [step_y] * 3 + [blank], 0).T.astype(BF16)
    moved = dot(moved, moves_ref[...])
    x_re, x_im = moved[:, :angles], moved[:, angles : 2 * angles]
    y_re, y_im = moved[:, 2 * angles : 3 * angles], moved[:, 3 * angles :]
    for slot in (0, 2):
        phase[slot] = x_re * y_re - x_im * y_im
        phase[slot + 1] = x_re * y_im + x_im * y_re
    mics = ctf_ref.shape[0] // cycles
    held_rows = table.shape[0] // (cycles + PAD)
    picked = picks(held_rows, owner_ref[...] * mics + mic_ref[...]).T.astype(BF16)

    steps = max(layers, 1)
    span = count // steps

    for hop in range(steps):

        @pl.loop(0, span // 4)
        def _(group):
            for u in range(4):
                spread_image(hop * span + group * 4 + u)

        if hop + 1 < layers:
            ctf_along(hop + 1)
    for hop in range(layers):
        ctf_over(hop)
    for hop in range(1, layers):
        refs_along(hop)

    chosen = picks(16, prior_ref[...])
    chosen = jnp.concatenate([chosen, chosen, chosen, jnp.zeros_like(chosen)], 0).astype(BF16)
    turn = dot(turns_ref[...], chosen)
    turn_re, turn_im = turn[:angles], turn[angles:]
    ctf_finish()

    table[...] = jnp.zeros_like(table)

    @pl.loop(0, devices)
    def _(block):
        for mic in range(mics):
            row = pl.multiple_of((block * mics + mic) * (cycles + PAD), 8)
            rows = all_ctf[block, mic * cycles : (mic + 1) * cycles, :]
            table[pl.ds(row, cycles), :] = rows.astype(F32)

    def put(values, start):
        re, im = values[:angles], values[angles:]
        spec[pl.ds(start, angles, stride=deep), :] = re * turn_re - im * turn_im
        spec[pl.ds(2 * cycles + start, angles, stride=deep), :] = re * turn_im + im * turn_re

    def transform(p):
        lines, powers = [], []
        w_re, w_im = phase[2], phase[3]
        t_re, t_im = phase[0], phase[1]
        for u in range(2):
            row = pl.multiple_of((p + u) * lane_rows, 8)
            scale = dot(picked, table[pl.ds(p + u, held_rows, stride=cycles + PAD), :].astype(BF16))
            a_re = work[pl.ds(row, count), :] * scale
            a_im = work[pl.ds(pl.multiple_of(plane + (p + u) * lane_rows, 8), count), :] * scale
            re, im = a_re * t_re - a_im * t_im, a_re * t_im + a_im * t_re
            t_re, t_im = t_re * w_re - t_im * w_im, t_re * w_im + t_im * w_re
            lines.append(jnp.concatenate([re, im], 1))
            powers.append(scale * scale)
        phase[0] = t_re
        phase[1] = t_im
        high, low = halves(jnp.concatenate(lines, 0))
        values = dot_nt(forward_ref[0], high) + dot_nt(forward_ref[1], high)
        values = values + dot_nt(forward_ref[0], low)
        put(values[:, :count], p)
        put(values[:, count:], p + 1)
        high, low = halves(jnp.concatenate(powers, 0))
        both = power_ref[...]
        values = dot_nt(both, jnp.concatenate([high, high], 1))
        values = values + dot_nt(both[:, :angles], low)
        put(values[:, :count], cycles + p)
        put(values[:, count:], cycles + p + 1)

    part = cycles // steps
    for hop in range(steps):

        @pl.loop(0, part // 2)
        def _(group):
            transform(hop * part + group * 2)

        refs_over(hop)
    refs_finish()

    def position(k):
        return (k % 2) * (classes // 2) + ((k // 2) % 2) * (classes // 4) + k // 4

    def place_ref(k):
        value = all_refs[k].astype(F32)
        lane = lax.broadcasted_iota(jnp.int32, value.shape, 1)
        swapped = pltpu.roll(value, depth // 2, 1)
        swapped = jnp.where(lane < depth // 2, swapped, -swapped)
        refs[pl.ds(position(k), angles, stride=pairs), :] = value
        refs[pl.ds(classes + position(k), angles, stride=pairs), :] = swapped

    @pl.loop(0, classes // 2)
    def _(group):
        for u in range(2):
            place_ref(group * 2 + u)

    def correlate(m):
        held = spec[pl.ds(pl.multiple_of(m * deep, 8), depth), :].astype(BF16)
        rows = pl.ds(pl.multiple_of(m * pairs, 8), 2 * classes)
        mixed[pl.ds(m, 2 * classes, stride=tall), :] = dot(refs[rows, :].astype(BF16), held)

    @pl.loop(0, angles // 8)
    def _(group):
        for u in range(8):
            correlate(group * 8 + u)

    valid = lax.broadcasted_iota(jnp.int32, (ROWS, count), 0) < ROTS

    def score(k, peak):
        re = mixed[pl.ds(pl.multiple_of(k * tall, 8), angles), :]
        im = mixed[pl.ds(pl.multiple_of((classes + k) * tall, 8), angles), :]
        high, low = halves(jnp.concatenate([re, im], 0))
        r_high, r_low = rotate_ref[0], rotate_ref[1]
        value = (dot(r_high, high) + dot(r_low, high) + dot(r_high, low)) * (1.0 / angles)
        value = jnp.where(valid, value, -jnp.inf)
        work[pl.ds(pl.multiple_of(k * ROWS, 8), ROWS), :] = value
        return jnp.maximum(peak, value)

    def score_four(group, peak):
        for u in range(4):
            peak = score(group * 4 + u, peak)
        return peak

    peak = lax.fori_loop(0, classes // 4, score_four, jnp.full((ROWS, count), -jnp.inf, F32))
    peak = jnp.max(peak, axis=0, keepdims=True)

    def expo(k, total):
        rows = pl.ds(pl.multiple_of(k * ROWS, 8), ROWS)
        value = jnp.exp(work[rows, :] - peak)
        work[rows, :] = value
        return total + value

    total = lax.fori_loop(0, classes, expo, jnp.zeros((ROWS, count), F32))
    total = jnp.sum(total, axis=0, keepdims=True)
    evid_ref[...] = peak + jnp.log(total)
    share = 1.0 / total

    def unrotate(k):
        row = position(k)
        weights = work[pl.ds(pl.multiple_of(row * ROWS, 8), ROWS), :] * share
        post_ref[pl.ds(k, 1), :] = jnp.sum(weights, axis=0, keepdims=True)
        high, low = halves(weights)
        stacked = jnp.concatenate(
            [high.astype(F32), high.astype(F32), low.astype(F32), jnp.zeros((8, count), F32)], 0
        ).astype(BF16)
        value = dot(spread_ref[...], stacked)
        refs[pl.ds(row, angles, stride=pairs), :] = value[:angles]
        refs[pl.ds(classes + row, angles, stride=pairs), :] = value[angles:]

    @pl.loop(0, classes // 4)
    def _(group):
        for u in range(4):
            unrotate(group * 4 + u)

    def gather_up(number, step):
        m = number * chunk + step
        held = spec[pl.ds(pl.multiple_of(m * deep, 8), depth), :]
        other = jnp.concatenate([-held[depth // 2 :], held[: depth // 2]], 0)
        right = jnp.concatenate([held, other], 1).astype(BF16)
        spun = refs[pl.ds(pl.multiple_of(m * pairs, 8), 2 * classes), :]
        left = jnp.concatenate([spun[:classes], spun[classes:]], 1).astype(BF16)
        parts.at[number][pl.ds(step, classes, stride=wide), :] = dot_nt(left, right)

    half, quarter = classes // 2 * wide, classes // 4 * wide

    def near_rows(number, flip, place):
        place = pl.multiple_of(flip * quarter + place * wide, 8)
        mine = pl.multiple_of(core * half + place, 8)
        return parts[number, pl.ds(mine, chunk), :] + near[number, pl.ds(place, chunk), :]

    first, second, third = {}, {}, {}

    def stage_near(number):
        start = pl.multiple_of((1 - core) * half, 8)
        first[number] = push(
            parts.at[number, pl.ds(start, half)],
            near.at[number],
            near_sems.at[0, number],
            near_sems.at[1, number],
            sibling,
        )

    def stage_side(number):
        first[number].wait_recv()
        for place in range(layers):
            side_out[number, place] = near_rows(number, 1 - side, place)
        second[number] = push(
            side_out.at[number],
            side_in.at[number],
            side_sems.at[0, number],
            side_sems.at[1, number],
            beside,
        )

    def stage_layer(number):
        second[number].wait_recv()
        for hop, place in enumerate(places):
            layer_out[number, hop] = near_rows(number, side, place) + side_in[number, place]
            if hop:
                third[number, hop] = push(
                    layer_out.at[number, hop],
                    layer_in.at[number, hop],
                    layer_sems.at[0, number, hop],
                    layer_sems.at[1, number, hop],
                    place * 4 + column,
                )

    def stage_total(number):
        total = layer_out[number, 0]
        for hop in range(1, layers):
            third[number, hop].wait_recv()
            total = total + layer_in[number, hop]
        return total

    parts[...] = jnp.zeros_like(parts)
    for number in range(CHUNKS):

        @pl.loop(0, chunk // 8)
        def _(group):
            for u in range(8):
                gather_up(number, group * 8 + u)

        stage_near(number)
        if number >= 1:
            stage_side(number - 1)
        if number >= 2:
            stage_layer(number - 2)
    stage_side(CHUNKS - 1)
    if CHUNKS >= 2:
        stage_layer(CHUNKS - 2)
    stage_layer(CHUNKS - 1)
    turned = jnp.concatenate([stage_total(number) for number in range(CHUNKS)], 0).T
    numer_ref[0, :, :angles] = turned[:cycles]
    denom_ref[0, :, :angles] = turned[cycles : 2 * cycles]
    numer_ref[0, :, angles:] = turned[2 * cycles : 3 * cycles]
    denom_ref[0, :, angles:] = turned[3 * cycles :]
    for copy in waiting:
        copy.wait_send()


def three(values):
    pieces = []
    rest = values.astype(np.float64)
    for _ in range(3):
        piece = rest.astype(np.float32).astype(BF16)
        pieces.append(piece)
        rest = rest - piece.astype(np.float64)
    return pieces


def run_fused(particles, owner, mic_local, shifts, prior, refs, ctf, devices):
    count, cycles, angles = particles.shape[0], particles.shape[1], particles.shape[2] // 2
    classes = devices
    layers = devices // 4
    mics = ctf.shape[0]
    depth = 4 * cycles
    forward, rotate, moves, order = tables(angles, cycles)
    chunk = angles // CHUNKS
    wide = chunk + PAD
    forward_high, forward_low = split_table(forward.T)
    rotate_high, rotate_low = split_table(rotate)
    rows = -(-devices * mics // 128) * 128
    theta = 2.0 * np.pi * np.arange(16) / 360.0
    spin = order[:, None] * theta[None, :]
    turns = np.concatenate([np.cos(spin), np.sin(spin)], 0)
    moving = np.zeros((128, 4 * angles), np.float32).astype(BF16)
    for axis in range(2):
        found = three(moves[axis][:, 0])
        for number, piece in enumerate(found):
            start = 48 * axis + 16 * number
            moving[start : start + 2 * SHIFT + 1, axis * 2 * angles :][:, : 2 * angles] = piece
    pieces = three(turns)
    constants = (
        moving,
        np.concatenate(pieces + [np.zeros_like(pieces[0])], 1),
        np.stack([forward_high, forward_low]),
        np.concatenate([forward_high[:, :angles], forward_low[:, :angles]], 1),
        np.stack([rotate_high.T, rotate_low.T]),
        np.concatenate(
            [rotate_high, rotate_low, rotate_high, np.zeros((2 * angles, 8), BF16)], 1
        ),
    )
    sums = jax.ShapeDtypeStruct((1, cycles, 2 * angles), F32)
    dma = pltpu.SemaphoreType.DMA
    post, evidence, numer, denom = pl.pallas_call(
        functools.partial(fused_kernel, (devices, count, cycles, angles)),
        out_shape=(
            jax.ShapeDtypeStruct((classes, count), F32),
            jax.ShapeDtypeStruct((1, count), F32),
            sums,
            sums,
        ),
        in_specs=[VMEM] * 13,
        out_specs=(VMEM,) * 4,
        scratch_shapes=[
            pltpu.VMEM((devices, mics * cycles, angles), BF16),
            pltpu.VMEM((devices, angles, depth), BF16),
            pltpu.VMEM((angles, depth), BF16),
            pltpu.VMEM((2 * cycles * (count + PAD), angles), F32),
            pltpu.VMEM((rows * (cycles + PAD), angles), F32),
            pltpu.VMEM((4, count, angles), F32),
            pltpu.VMEM((angles * (depth + PAD), count), F32),
            pltpu.VMEM((angles * (2 * classes + PAD), count), F32),
            pltpu.VMEM((2 * classes * (angles + PAD), count), F32),
            pltpu.VMEM((CHUNKS, classes * wide, depth), F32),
            pltpu.VMEM((CHUNKS, classes // 2 * wide, depth), F32),
            pltpu.VMEM((CHUNKS, layers, chunk, depth), F32),
            pltpu.VMEM((CHUNKS, layers, chunk, depth), F32),
            pltpu.VMEM((CHUNKS, layers, chunk, depth), F32),
            pltpu.VMEM((CHUNKS, layers, chunk, depth), F32),
            dma((devices,)),
            dma((devices,)),
            dma((devices,)),
            dma((devices,)),
            dma((2, CHUNKS)),
            dma((2, CHUNKS)),
            dma((2, CHUNKS, layers)),
        ],
        compiler_params=pltpu.CompilerParams(
            collective_id=2, has_side_effects=True, vmem_limit_bytes=60 * MIB
        ),
    )(owner.reshape(1, count), mic_local.reshape(1, count), shifts.T, particles, ctf.reshape(mics * cycles, angles), refs,
      prior.reshape(1, count), *[jnp.asarray(constant) for constant in constants])
    return post.T, evidence[0], numer, denom


def per_device(particles, owner, mic_local, shifts, prior, refs, ctf):
    devices = lax.axis_size("blk")
    count, cycles, angles = particles.shape[0], particles.shape[1], particles.shape[2] // 2
    local = refs.shape[0]
    classes = local * devices
    mics = ctf.shape[0]
    if local == 1 and classes <= 32:
        return run_fused(particles, owner, mic_local, shifts, prior, refs, ctf, devices)
    forward, rotate, moves, order = tables(angles, cycles)

    values = refs.astype(F32)
    table = jnp.asarray(forward.astype(np.float32))
    spectra = jnp.matmul(values, table, precision=HIGH).astype(BF16)
    power = values[..., :angles] ** 2 + values[..., angles:] ** 2
    power_spectra = jnp.matmul(power, table[:angles], precision=HIGH).astype(BF16)
    both = jnp.stack([spectra, -0.5 * power_spectra], 1).reshape(local, 2, cycles, 2, angles)
    both = both.transpose(0, 4, 3, 1, 2).reshape(local * angles, 4 * cycles)
    own = jnp.concatenate([ctf.reshape(mics * cycles, angles), both.astype(BF16)], 0)
    everything = gather_blocks(own, devices)

    index = jnp.stack([owner[:, 0], mic_local, shifts[:, 0], shifts[:, 1]])
    theta = 2.0 * jnp.pi * prior.astype(F32) / 360.0
    spin = jnp.asarray(order.astype(np.float32))[:, None] * theta[None, :]
    turn = jnp.concatenate([jnp.cos(spin), jnp.sin(spin)], 0)
    forward_t = jnp.asarray(np.stack(split_table(forward.T)))
    rotate_high, rotate_low = split_table(rotate)
    rotate_t = jnp.asarray(np.stack([rotate_high.T, rotate_low.T]))
    spread = jnp.asarray(
        np.concatenate(
            [rotate_high, rotate_low, rotate_high, np.zeros((2 * angles, 8), BF16)], 1
        )
    )
    post, evidence, parts = pl.pallas_call(
        functools.partial(score_kernel, (count, cycles, angles, classes, mics)),
        out_shape=(
            jax.ShapeDtypeStruct((classes, count), F32),
            jax.ShapeDtypeStruct((1, count), F32),
            jax.ShapeDtypeStruct((2 * classes * angles, 4 * cycles), F32),
        ),
        in_specs=[SMEM] + [VMEM] * 8,
        out_specs=(VMEM, VMEM, VMEM),
        scratch_shapes=[
            pltpu.VMEM((3 * cycles * count, angles), F32),
            pltpu.VMEM((angles * 4 * cycles, count), F32),
            pltpu.VMEM((2 * classes * angles, count), F32),
        ],
        compiler_params=pltpu.CompilerParams(vmem_limit_bytes=63 * MIB),
    )(index, particles, everything, jnp.asarray(moves[0], F32), jnp.asarray(moves[1], F32), turn,
      forward_t, rotate_t, spread)
    numer, denom = reduce_blocks(parts[: classes * angles], devices, local, cycles, angles)
    return post.T, evidence[0], numer, denom


def solution(mesh):
    in_specs = (
        P(("groups", "blk"), None, None),
        P(("groups", "blk"), None),
        P(("groups", "blk")),
        P(("groups", "blk"), None),
        P(("groups", "blk")),
        P(("groups", "blk"), None, None),
        P(("groups", "blk"), None, None),
    )
    out_specs = (
        P(("groups", "blk"), None),
        P(("groups", "blk")),
        P(("groups", "blk"), None, None),
        P(("groups", "blk"), None, None),
    )
    return jax.shard_map(
        per_device, mesh=mesh, in_specs=in_specs, out_specs=out_specs, check_vma=False
    )
```

```python
import functools

import jax
import jax.numpy as jnp
import numpy as np
from jax import lax
from jax.experimental import pallas as pl
from jax.experimental.pallas import tpu as pltpu
from jax.sharding import PartitionSpec as P

BOX = 128
ROTS = 36
ROWS = 40
SHIFT = 5
HIGH = lax.Precision.HIGHEST
MESH = pl.DeviceIdType.MESH
F32 = jnp.float32
BF16 = jnp.bfloat16
VMEM = pl.BlockSpec(memory_space=pltpu.VMEM)
SMEM = pl.BlockSpec(memory_space=pltpu.SMEM)
MIB = 1 << 20
PAD = 8
CHUNKS = 4


def split_table(table):
    high = table.astype(np.float32).astype(BF16)
    low = (table - high.astype(np.float64)).astype(np.float32).astype(BF16)
    return high, low


def tables(angles, cycles):
    sample = np.arange(angles)
    order = np.where(sample < angles // 2, sample, sample - angles)
    phase = 2.0 * np.pi * ((sample[:, None] * order[None, :]) % angles) / angles
    cosine, sine = np.cos(phase), np.sin(phase)
    forward = np.block([[cosine, -sine], [sine, cosine]])
    spin = 2.0 * np.pi * ((order[:, None] * np.arange(ROTS)[None, :]) % ROTS) / ROTS
    rotate = np.zeros((2 * angles, ROWS))
    rotate[:, :ROTS] = np.concatenate([np.cos(spin), np.sin(spin)], 0)
    azimuth = 2.0 * np.pi * sample / angles
    step = np.arange(-SHIFT, SHIFT + 1)[:, None, None] * np.arange(1, cycles + 1)[None, :, None]
    moves = []
    for part in (np.cos(azimuth), np.sin(azimuth)):
        turn = -2.0 * np.pi / BOX * step * part[None, None, :]
        moves.append(np.concatenate([np.cos(turn), np.sin(turn)], -1))
    return forward, rotate, moves, order


def neighbours(devices):
    me = lax.axis_index("blk")
    core = lax.rem(me, 2)
    side = lax.rem(me // 2, 2)
    layer = me // 4
    return me, core, side, layer, devices // 4


def greet(partners):
    barrier = pltpu.get_barrier_semaphore()
    for partner in partners:
        pl.semaphore_signal(barrier, inc=1, device_id={"blk": partner}, device_id_type=MESH)
    pl.semaphore_wait(barrier, len(partners))


def gather_kernel(devices, own_ref, all_ref, send_sem, recv_sem):
    me, core, side, layer, layers = neighbours(devices)
    column = side * 2 + core
    across = (1 - side) * 2 + core
    sibling = me + 1 - 2 * core
    beside = me + 2 - 4 * side
    others = [lax.rem(layer + hop, layers) for hop in range(1, layers)]
    greet([other * 4 + column for other in others] + [sibling, beside])
    sent = []

    def send(source, block, target, slot):
        copy = pltpu.make_async_remote_copy(
            src_ref=source,
            dst_ref=all_ref.at[block],
            send_sem=send_sem.at[slot],
            recv_sem=recv_sem.at[block],
            device_id={"blk": target},
            device_id_type=MESH,
        )
        copy.start()
        sent.append(copy)

    def arrive(block):
        pltpu.make_async_remote_copy(
            src_ref=own_ref,
            dst_ref=all_ref.at[block],
            send_sem=send_sem.at[0],
            recv_sem=recv_sem.at[block],
            device_id={"blk": sibling},
            device_id_type=MESH,
        ).wait_recv()

    for hop, other in enumerate(others):
        send(own_ref, me, other * 4 + column, hop)
    send(own_ref, me, beside, layers)
    send(own_ref, me, sibling, 2 * layers)
    all_ref[me] = own_ref[...]
    far = me + 2 - 4 * side
    for hop in range(layers):
        if hop > 0:
            block = others[hop - 1] * 4 + column
            arrive(block)
            send(all_ref.at[block], block, beside, layers + hop)
            send(all_ref.at[block], block, sibling, 2 * layers + hop)
        far = (layer if hop == 0 else others[hop - 1]) * 4 + across
        arrive(far)
        send(all_ref.at[far], far, sibling, 3 * layers + hop)
    for hop in range(layers):
        place = (layer if hop == 0 else others[hop - 1]) * 4
        arrive(place + side * 2 + 1 - core)
        arrive(place + (1 - side) * 2 + 1 - core)
    for copy in sent:
        copy.wait_send()


def gather_blocks(own, devices):
    return pl.pallas_call(
        functools.partial(gather_kernel, devices),
        out_shape=jax.ShapeDtypeStruct((devices,) + own.shape, own.dtype),
        in_specs=[VMEM],
        out_specs=VMEM,
        scratch_shapes=[
            pltpu.SemaphoreType.DMA((devices,)),
            pltpu.SemaphoreType.DMA((devices,)),
        ],
        compiler_params=pltpu.CompilerParams(
            collective_id=0, has_side_effects=True, vmem_limit_bytes=48 * MIB
        ),
    )(own)


def reduce_kernel(devices, local, part_ref, numer_ref, denom_ref, *scratch):
    near, side_in, layer_in, side_out, layer_out, send_sem, near_sem, side_sem, layer_sem = scratch
    me, core, side, layer, layers = neighbours(devices)
    column = side * 2 + core
    sibling = me + 1 - 2 * core
    beside = me + 2 - 4 * side
    depth = part_ref.shape[0] // devices
    others = [lax.rem(layer + hop, layers) for hop in range(1, layers)]
    hops = list(range(1, layers)) + [0]
    greet([other * 4 + column for other in others] + [sibling, beside])

    def rows(block):
        return pl.ds(pl.multiple_of(block * depth, depth), depth)

    def target(hop):
        return layer if hop == 0 else others[hop - 1]

    def copy_to(source, sink, number, sem, device):
        return pltpu.make_async_remote_copy(
            src_ref=source,
            dst_ref=sink,
            send_sem=send_sem.at[number],
            recv_sem=sem,
            device_id={"blk": device},
            device_id_type=MESH,
        )

    first, second, third = {}, {}, {}
    for hop in hops:
        for flip in (1, 0):
            place = jnp.where(side == 1, 1 - flip, flip) if flip else side
            block = target(hop) * 4 + place * 2 + 1 - core
            slot = 2 * hop + flip
            first[slot] = copy_to(
                part_ref.at[rows(block)], near.at[slot], slot, near_sem.at[slot], sibling
            )
            first[slot].start()
    for hop in hops:
        first[2 * hop + 1].wait_recv()
        block = target(hop) * 4 + (1 - side) * 2 + core
        side_out[hop] = part_ref[rows(block), :] + near[2 * hop + 1]
        second[hop] = copy_to(
            side_out.at[hop], side_in.at[hop], 2 * layers + hop, side_sem.at[hop], beside
        )
        second[hop].start()
    for hop in hops:
        first[2 * hop].wait_recv()
        second[hop].wait_recv()
        block = target(hop) * 4 + column
        layer_out[hop] = part_ref[rows(block), :] + near[2 * hop] + side_in[hop]
        if hop:
            third[hop] = copy_to(
                layer_out.at[hop],
                layer_in.at[hop],
                3 * layers + hop,
                layer_sem.at[hop],
                target(hop) * 4 + column,
            )
            third[hop].start()
    total = layer_out[0]
    for hop in range(1, layers):
        third[hop].wait_recv()
        total = total + layer_in[hop]
    cycles, angles = numer_ref.shape[1], numer_ref.shape[2] // 2
    for item in range(local):
        turned = total[item * angles : (item + 1) * angles].T
        numer_ref[item, :, :angles] = turned[:cycles]
        denom_ref[item, :, :angles] = turned[cycles : 2 * cycles]
        numer_ref[item, :, angles:] = turned[2 * cycles : 3 * cycles]
        denom_ref[item, :, angles:] = turned[3 * cycles :]
    for copies in (first, second, third):
        for copy in copies.values():
            copy.wait_send()


def reduce_blocks(parts, devices, local, cycles, angles):
    layers = devices // 4
    depth = local * angles
    lanes = parts.shape[1]
    shape = jax.ShapeDtypeStruct((local, cycles, 2 * angles), F32)
    return pl.pallas_call(
        functools.partial(reduce_kernel, devices, local),
        out_shape=(shape, shape),
        in_specs=[VMEM],
        out_specs=(VMEM, VMEM),
        scratch_shapes=[
            pltpu.VMEM((2 * layers, depth, lanes), F32),
            pltpu.VMEM((layers, depth, lanes), F32),
            pltpu.VMEM((layers, depth, lanes), F32),
            pltpu.VMEM((layers, depth, lanes), F32),
            pltpu.VMEM((layers, depth, lanes), F32),
            pltpu.SemaphoreType.DMA((4 * layers,)),
            pltpu.SemaphoreType.DMA((2 * layers,)),
            pltpu.SemaphoreType.DMA((layers,)),
            pltpu.SemaphoreType.DMA((layers,)),
        ],
        compiler_params=pltpu.CompilerParams(
            collective_id=1, has_side_effects=True, vmem_limit_bytes=48 * MIB
        ),
    )(parts)


def halves(value):
    high = value.astype(BF16)
    return high, (value - high.astype(F32)).astype(BF16)


def dot(left, right):
    return jnp.dot(left, right, preferred_element_type=F32)


def dot_nt(left, right):
    return lax.dot_general(left, right, (((1,), (1,)), ((), ())), preferred_element_type=F32)


def score_kernel(sizes, index_ref, images_ref, all_ref, move_x_ref, move_y_ref, turn_ref,
                 forward_ref, rotate_ref, spread_ref, post_ref, evid_ref, parts_ref,
                 work, spec, refs):
    count, cycles, angles, classes, mics = sizes
    depth = 4 * cycles
    plane = cycles * count

    def shift_one(i):
        own, mic = index_ref[0, i], index_ref[1, i]
        move_x, move_y = move_x_ref[index_ref[2, i] + SHIFT], move_y_ref[index_ref[3, i] + SHIFT]
        row = pl.multiple_of(mic * cycles, cycles)
        transfer = all_ref[own, pl.ds(row, cycles), :].astype(F32)
        image = images_ref[i].astype(F32)
        x_re, x_im = move_x[:, :angles], move_x[:, angles:]
        y_re, y_im = move_y[:, :angles], move_y[:, angles:]
        re = x_re * y_re - x_im * y_im
        im = x_re * y_im + x_im * y_re
        a_re, a_im = image[:, :angles], image[:, angles:]
        work[pl.ds(i, cycles, stride=count), :] = transfer * (a_re * re - a_im * im)
        work[pl.ds(plane + i, cycles, stride=count), :] = transfer * (a_re * im + a_im * re)
        work[pl.ds(2 * plane + i, cycles, stride=count), :] = transfer * transfer

    @pl.loop(0, count // 4)
    def _(group):
        for u in range(4):
            shift_one(group * 4 + u)

    def place_ref(k):
        base = mics * cycles
        half = all_ref[k // sizes_local, pl.ds(base + (k % sizes_local) * angles, angles), :]
        value = half.astype(F32)
        lane = lax.broadcasted_iota(jnp.int32, value.shape, 1)
        swapped = pltpu.roll(value, depth // 2, 1)
        swapped = jnp.where(lane < depth // 2, swapped, -swapped)
        refs[pl.ds(k, angles, stride=2 * classes), :] = value
        refs[pl.ds(classes + k, angles, stride=2 * classes), :] = swapped

    sizes_local = classes // all_ref.shape[0]

    @pl.loop(0, classes // 2)
    def _(group):
        for u in range(2):
            place_ref(group * 2 + u)

    turn_re, turn_im = turn_ref[:angles], turn_ref[angles:]

    def put(values, start):
        re, im = values[:angles], values[angles:]
        spec[pl.ds(start, angles, stride=depth), :] = re * turn_re - im * turn_im
        spec[pl.ds(2 * cycles + start, angles, stride=depth), :] = re * turn_im + im * turn_re

    def transform(p):
        rows = pl.ds(pl.multiple_of(p * count, count), count)
        re = work[rows, :]
        im = work[pl.ds(pl.multiple_of(plane + p * count, count), count), :]
        power = work[pl.ds(pl.multiple_of(2 * plane + p * count, count), count), :]
        high, low = halves(jnp.concatenate([re, im], 1))
        f_high, f_low = forward_ref[0], forward_ref[1]
        values = dot_nt(f_high, high) + dot_nt(f_low, high) + dot_nt(f_high, low)
        put(values, p)
        high, low = halves(power)
        f_high, f_low = f_high[:, :angles], f_low[:, :angles]
        values = dot_nt(f_high, high) + dot_nt(f_low, high) + dot_nt(f_high, low)
        put(values, cycles + p)

    @pl.loop(0, cycles // 2)
    def _(group):
        for u in range(2):
            transform(group * 2 + u)

    def correlate(m):
        held = spec[pl.ds(pl.multiple_of(m * depth, depth), depth), :].astype(BF16)
        rows = pl.ds(pl.multiple_of(m * 2 * classes, 2 * classes), 2 * classes)
        parts_ref[pl.ds(m, 2 * classes, stride=angles), :] = dot(refs[rows, :].astype(BF16), held)

    @pl.loop(0, angles // 8)
    def _(group):
        for u in range(8):
            correlate(group * 8 + u)

    scale = 1.0 / angles
    valid = lax.broadcasted_iota(jnp.int32, (ROWS, count), 0) < ROTS

    def score(k, peak):
        re = parts_ref[pl.ds(pl.multiple_of(k * angles, angles), angles), :]
        im = parts_ref[pl.ds(pl.multiple_of((classes + k) * angles, angles), angles), :]
        high, low = halves(jnp.concatenate([re, im], 0))
        r_high, r_low = rotate_ref[0], rotate_ref[1]
        value = (dot(r_high, high) + dot(r_low, high) + dot(r_high, low)) * scale
        value = jnp.where(valid, value, -jnp.inf)
        work[pl.ds(pl.multiple_of(k * ROWS, 8), ROWS), :] = value
        return jnp.maximum(peak, value)

    def score_two(group, peak):
        return score(group * 2 + 1, score(group * 2, peak))

    peak = lax.fori_loop(0, classes // 2, score_two, jnp.full((ROWS, count), -jnp.inf, F32))
    peak = jnp.max(peak, axis=0, keepdims=True)

    def expo(k, total):
        rows = pl.ds(pl.multiple_of(k * ROWS, 8), ROWS)
        value = jnp.exp(work[rows, :] - peak)
        work[rows, :] = value
        return total + value

    total = lax.fori_loop(0, classes, expo, jnp.zeros((ROWS, count), F32))
    total = jnp.sum(total, axis=0, keepdims=True)
    evid_ref[...] = peak + jnp.log(total)
    share = 1.0 / total

    def unrotate(k):
        weights = work[pl.ds(pl.multiple_of(k * ROWS, 8), ROWS), :] * share
        post_ref[pl.ds(k, 1), :] = jnp.sum(weights, axis=0, keepdims=True)
        high, low = halves(weights)
        stacked = jnp.concatenate(
            [high.astype(F32), high.astype(F32), low.astype(F32), jnp.zeros((8, count), F32)], 0
        ).astype(BF16)
        value = dot(spread_ref[...], stacked)
        refs[pl.ds(k, angles, stride=2 * classes), :] = value[:angles]
        refs[pl.ds(classes + k, angles, stride=2 * classes), :] = value[angles:]

    @pl.loop(0, classes // 2)
    def _(group):
        for u in range(2):
            unrotate(group * 2 + u)

    def gather_up(m):
        held = spec[pl.ds(pl.multiple_of(m * depth, depth), depth), :]
        other = jnp.concatenate([-held[depth // 2 :], held[: depth // 2]], 0)
        right = jnp.concatenate([held, other], 1).astype(BF16)
        rows = pl.ds(pl.multiple_of(m * 2 * classes, 2 * classes), 2 * classes)
        spun = refs[rows, :]
        left = jnp.concatenate([spun[:classes], spun[classes:]], 1).astype(BF16)
        parts_ref[pl.ds(m, classes, stride=angles), :] = dot_nt(left, right)

    @pl.loop(0, angles // 8)
    def _(group):
        for u in range(8):
            gather_up(group * 8 + u)


def fused_kernel(sizes, owner_ref, mic_ref, shift_ref, particles_ref, ctf_ref, own_values_ref,
                 prior_ref, moves_ref, turns_ref, forward_ref, power_ref,
                 rotate_ref, spread_ref, post_ref, evid_ref, total_ref,
                 images_ref, images_sem, all_ctf, all_refs, own_refs, work, table, phase, spec, refs, mixed, parts,
                 near, side_out, side_in, layer_out, layer_in,
                 ctf_send, ctf_recv, refs_send, refs_recv, near_sems, side_sems, layer_sems):
    devices, count, cycles, angles = sizes
    classes = devices
    depth = 4 * cycles
    lane_rows, deep, pairs, tall = count + PAD, depth + PAD, 2 * classes + PAD, angles + PAD
    plane = cycles * lane_rows
    chunk = angles // CHUNKS
    wide = chunk + PAD

    fetch = pltpu.make_async_copy(particles_ref, images_ref, images_sem)
    fetch.start()
    me, core, side, layer, layers = neighbours(devices)
    column = side * 2 + core
    sibling = me + 1 - 2 * core
    beside = me + 2 - 4 * side
    others = [lax.rem(layer + hop, layers) for hop in range(1, layers)]
    places = [layer] + others
    greet([other * 4 + column for other in others] + [sibling, beside])
    waiting = []

    def push(source, sink, send_sem, recv_sem, device):
        copy = pltpu.make_async_remote_copy(
            src_ref=source,
            dst_ref=sink,
            send_sem=send_sem,
            recv_sem=recv_sem,
            device_id={"blk": device},
            device_id_type=MESH,
        )
        copy.start()
        waiting.append(copy)
        return copy

    def spreader(own, everything, sends, recvs):
        def send(source, block, device, slot):
            push(source, everything.at[block], sends.at[slot], recvs.at[block], device)

        def arrive(block):
            pltpu.make_async_remote_copy(
                src_ref=own,
                dst_ref=everything.at[block],
                send_sem=sends.at[0],
                recv_sem=recvs.at[block],
                device_id={"blk": sibling},
                device_id_type=MESH,
            ).wait_recv()

        def begin():
            for hop, other in enumerate(others):
                send(own, me, other * 4 + column, hop)
            send(own, me, beside, layers)
            send(own, me, sibling, 2 * layers)

        def along(hop):
            block = places[hop] * 4 + column
            arrive(block)
            send(everything.at[block], block, beside, layers + hop)
            send(everything.at[block], block, sibling, 2 * layers + hop)

        def over(hop):
            block = places[hop] * 4 + (1 - side) * 2 + core
            arrive(block)
            send(everything.at[block], block, sibling, 3 * layers + hop)

        def finish():
            for place in places:
                arrive(place * 4 + side * 2 + 1 - core)
                arrive(place * 4 + (1 - side) * 2 + 1 - core)

        return begin, along, over, finish

    ctf_begin, ctf_along, ctf_over, ctf_finish = spreader(ctf_ref, all_ctf, ctf_send, ctf_recv)
    refs_begin, refs_along, refs_over, refs_finish = spreader(
        own_refs, all_refs, refs_send, refs_recv
    )

    ctf_begin()
    all_ctf[me] = ctf_ref[...]
    f_high, f_low = forward_ref[0], forward_ref[1]
    values = own_values_ref[0].astype(F32)
    v_re, v_im = values[:, :angles], values[:, angles:]
    halved = -0.5 * (v_re * v_re + v_im * v_im)
    none = jnp.zeros_like(halved)
    stacked = jnp.concatenate(
        [
            values,
            jnp.concatenate([halved, none], 1),
            jnp.concatenate([v_im, -v_re], 1),
            jnp.concatenate([none, -halved], 1),
        ],
        0,
    )
    high, low = halves(stacked)
    top, bottom = f_high[:angles], f_low[:angles]
    own_block = (dot_nt(top, high) + dot_nt(bottom, high) + dot_nt(top, low)).astype(BF16)
    own_refs[...] = own_block
    all_refs[me] = own_block
    refs_begin()
    table[...] = jnp.zeros_like(table)
    parts[...] = jnp.zeros_like(parts)
    fetch.wait()

    def spread_image(i):
        image = images_ref[i].astype(F32)
        work[pl.ds(i, cycles, stride=lane_rows), :] = image[:, :angles]
        work[pl.ds(plane + i, cycles, stride=lane_rows), :] = image[:, angles:]

    def picks(rows, line):
        return (lax.broadcasted_iota(jnp.int32, (rows, count), 0) == line).astype(F32)

    step_x, step_y = picks(16, shift_ref[0:1] + SHIFT), picks(16, shift_ref[1:2] + SHIFT)
    blank = jnp.zeros((32, count), F32)
    moved = jnp.concatenate([step_x] * 3 + [step_y] * 3 + [blank], 0).T.astype(BF16)
    moved = dot(moved, moves_ref[...])
    x_re, x_im = moved[:, :angles], moved[:, angles : 2 * angles]
    y_re, y_im = moved[:, 2 * angles : 3 * angles], moved[:, 3 * angles :]
    for slot in (0, 2):
        phase[slot] = x_re * y_re - x_im * y_im
        phase[slot + 1] = x_re * y_im + x_im * y_re
    mics = ctf_ref.shape[0] // cycles
    held_rows = table.shape[0] // (cycles + PAD)
    picked = picks(held_rows, owner_ref[...] * mics + mic_ref[...]).T.astype(BF16)

    chosen = picks(16, prior_ref[...])
    chosen = jnp.concatenate([chosen, chosen, chosen, jnp.zeros_like(chosen)], 0).astype(BF16)
    turn = dot(turns_ref[...], chosen)
    turn_re, turn_im = turn[:angles], turn[angles:]
    steps = max(layers, 1)
    span = count // steps

    for hop in range(steps):

        @pl.loop(0, span // 4)
        def _(group):
            for u in range(4):
                spread_image(hop * span + group * 4 + u)

        if hop + 1 < layers:
            ctf_along(hop + 1)
    for hop in range(layers):
        ctf_over(hop)
    ctf_finish()

    @pl.loop(0, devices)
    def _(block):
        for mic in range(mics):
            row = pl.multiple_of((block * mics + mic) * (cycles + PAD), 8)
            rows = all_ctf[block, mic * cycles : (mic + 1) * cycles, :]
            table[pl.ds(row, cycles), :] = rows.astype(F32)

    def put(values, start):
        re, im = values[:angles], values[angles:]
        spec[pl.ds(start, angles, stride=deep), :] = re * turn_re - im * turn_im
        spec[pl.ds(2 * cycles + start, angles, stride=deep), :] = re * turn_im + im * turn_re

    def transform(p):
        lines, powers = [], []
        w_re, w_im = phase[2], phase[3]
        t_re, t_im = phase[0], phase[1]
        for u in range(2):
            row = pl.multiple_of((p + u) * lane_rows, 8)
            scale = dot(picked, table[pl.ds(p + u, held_rows, stride=cycles + PAD), :].astype(BF16))
            a_re = work[pl.ds(row, count), :] * scale
            a_im = work[pl.ds(pl.multiple_of(plane + (p + u) * lane_rows, 8), count), :] * scale
            re, im = a_re * t_re - a_im * t_im, a_re * t_im + a_im * t_re
            t_re, t_im = t_re * w_re - t_im * w_im, t_re * w_im + t_im * w_re
            lines.append(jnp.concatenate([re, im], 1))
            powers.append(scale * scale)
        phase[0] = t_re
        phase[1] = t_im
        high, low = halves(jnp.concatenate(lines, 0))
        values = dot_nt(forward_ref[0], high) + dot_nt(forward_ref[1], high)
        values = values + dot_nt(forward_ref[0], low)
        put(values[:, :count], p)
        put(values[:, count:], p + 1)
        high, low = halves(jnp.concatenate(powers, 0))
        both = power_ref[...]
        values = dot_nt(both, jnp.concatenate([high, high], 1))
        values = values + dot_nt(both[:, :angles], low)
        put(values[:, :count], cycles + p)
        put(values[:, count:], cycles + p + 1)

    part = cycles // steps
    for hop in range(steps):

        @pl.loop(0, part // 2)
        def _(group):
            transform(hop * part + group * 2)

        if hop == 0:
            for other in range(1, layers):
                refs_along(other)
        if hop == max(steps - 2, 0):
            for other in range(layers // 2):
                refs_over(other)
    for other in range(layers // 2, layers):
        refs_over(other)
    refs_finish()

    def position(k):
        return (k % 2) * (classes // 2) + ((k // 2) % 2) * (classes // 4) + k // 4

    def place_ref(k):
        value = all_refs[k].astype(F32)
        lane = lax.broadcasted_iota(jnp.int32, value.shape, 1)
        swapped = pltpu.roll(value, depth // 2, 1)
        swapped = jnp.where(lane < depth // 2, swapped, -swapped)
        refs[pl.ds(position(k), angles, stride=pairs), :] = value
        refs[pl.ds(classes + position(k), angles, stride=pairs), :] = swapped

    @pl.loop(0, classes // 2)
    def _(group):
        for u in range(2):
            place_ref(group * 2 + u)

    def correlate(m):
        held = spec[pl.ds(pl.multiple_of(m * deep, 8), depth), :].astype(BF16)
        rows = pl.ds(pl.multiple_of(m * pairs, 8), 2 * classes)
        mixed[pl.ds(m, 2 * classes, stride=tall), :] = dot(refs[rows, :].astype(BF16), held)

    @pl.loop(0, angles // 8)
    def _(group):
        for u in range(8):
            correlate(group * 8 + u)

    valid = lax.broadcasted_iota(jnp.int32, (ROWS, count), 0) < ROTS

    def score(k, peak):
        re = mixed[pl.ds(pl.multiple_of(k * tall, 8), angles), :]
        im = mixed[pl.ds(pl.multiple_of((classes + k) * tall, 8), angles), :]
        high, low = halves(jnp.concatenate([re, im], 0))
        r_high, r_low = rotate_ref[0], rotate_ref[1]
        value = (dot(r_high, high) + dot(r_low, high) + dot(r_high, low)) * (1.0 / angles)
        value = jnp.where(valid, value, -jnp.inf)
        work[pl.ds(pl.multiple_of(k * ROWS, 8), ROWS), :] = value
        return jnp.maximum(peak, value)

    def score_four(group, peak):
        for u in range(4):
            peak = score(group * 4 + u, peak)
        return peak

    peak = lax.fori_loop(0, classes // 4, score_four, jnp.full((ROWS, count), -jnp.inf, F32))
    peak = jnp.max(peak, axis=0, keepdims=True)

    def expo(k, total):
        rows = pl.ds(pl.multiple_of(k * ROWS, 8), ROWS)
        value = jnp.exp(work[rows, :] - peak)
        work[rows, :] = value
        return total + value

    total = lax.fori_loop(0, classes, expo, jnp.zeros((ROWS, count), F32))
    total = jnp.sum(total, axis=0, keepdims=True)
    evid_ref[...] = peak + jnp.log(total)
    share = 1.0 / total

    def unrotate(k):
        row = position(k)
        weights = work[pl.ds(pl.multiple_of(row * ROWS, 8), ROWS), :] * share
        post_ref[pl.ds(k, 1), :] = jnp.sum(weights, axis=0, keepdims=True)
        high, low = halves(weights)
        stacked = jnp.concatenate(
            [high.astype(F32), high.astype(F32), low.astype(F32), jnp.zeros((8, count), F32)], 0
        ).astype(BF16)
        value = dot(spread_ref[...], stacked)
        refs[pl.ds(row, angles, stride=pairs), :] = value[:angles]
        refs[pl.ds(classes + row, angles, stride=pairs), :] = value[angles:]

    @pl.loop(0, classes // 4)
    def _(group):
        for u in range(4):
            unrotate(group * 4 + u)

    def gather_up(number, step):
        m = number * chunk + step
        held = spec[pl.ds(pl.multiple_of(m * deep, 8), depth), :]
        other = jnp.concatenate([-held[depth // 2 :], held[: depth // 2]], 0)
        right = jnp.concatenate([held, other], 1).astype(BF16)
        spun = refs[pl.ds(pl.multiple_of(m * pairs, 8), 2 * classes), :]
        left = jnp.concatenate([spun[:classes], spun[classes:]], 1).astype(BF16)
        parts.at[number][pl.ds(step, classes, stride=wide), :] = dot_nt(left, right)

    half, quarter = classes // 2 * wide, classes // 4 * wide

    def near_rows(number, flip, place):
        place = pl.multiple_of(flip * quarter + place * wide, 8)
        mine = pl.multiple_of(core * half + place, 8)
        return parts[number, pl.ds(mine, chunk), :] + near[number, pl.ds(place, chunk), :]

    first, second, third = {}, {}, {}

    def stage_near(number):
        start = pl.multiple_of((1 - core) * half, 8)
        first[number] = push(
            parts.at[number, pl.ds(start, half)],
            near.at[number],
            near_sems.at[0, number],
            near_sems.at[1, number],
            sibling,
        )

    def stage_side(number):
        first[number].wait_recv()
        for place in range(layers):
            side_out[number, place] = near_rows(number, 1 - side, place)
        second[number] = push(
            side_out.at[number],
            side_in.at[number],
            side_sems.at[0, number],
            side_sems.at[1, number],
            beside,
        )

    def stage_layer(number):
        second[number].wait_recv()
        for hop, place in enumerate(places):
            layer_out[number, hop] = near_rows(number, side, place) + side_in[number, place]
            if hop:
                third[number, hop] = push(
                    layer_out.at[number, hop],
                    layer_in.at[number, hop],
                    layer_sems.at[0, number, hop],
                    layer_sems.at[1, number, hop],
                    place * 4 + column,
                )

    def stage_total(number):
        total = layer_out[number, 0]
        for hop in range(1, layers):
            third[number, hop].wait_recv()
            total = total + layer_in[number, hop]
        return total

    for number in range(CHUNKS):

        @pl.loop(0, chunk // 8)
        def _(group):
            for u in range(8):
                gather_up(number, group * 8 + u)

        stage_near(number)
        if number >= 1:
            stage_side(number - 1)
        if number >= 2:
            stage_layer(number - 2)
    stage_side(CHUNKS - 1)
    if CHUNKS >= 2:
        stage_layer(CHUNKS - 2)
    stage_layer(CHUNKS - 1)
    for number in range(CHUNKS):
        total_ref[number * chunk : (number + 1) * chunk] = stage_total(number)
    for copy in waiting:
        copy.wait_send()


def finish_kernel(post_in, evid_in, total_ref, post_ref, evid_ref, numer_ref, denom_ref):
    cycles, angles = numer_ref.shape[1], numer_ref.shape[2] // 2
    post_ref[...] = post_in[...]
    evid_ref[...] = evid_in[...]
    turned = total_ref[...].T
    numer_ref[0, :, :angles] = turned[:cycles]
    denom_ref[0, :, :angles] = turned[cycles : 2 * cycles]
    numer_ref[0, :, angles:] = turned[2 * cycles : 3 * cycles]
    denom_ref[0, :, angles:] = turned[3 * cycles :]


def three(values):
    pieces = []
    rest = values.astype(np.float64)
    for _ in range(3):
        piece = rest.astype(np.float32).astype(BF16)
        pieces.append(piece)
        rest = rest - piece.astype(np.float64)
    return pieces


def run_fused(particles, owner, mic_local, shifts, prior, refs, ctf, devices):
    count, cycles, angles = particles.shape[0], particles.shape[1], particles.shape[2] // 2
    classes = devices
    layers = devices // 4
    mics = ctf.shape[0]
    depth = 4 * cycles
    forward, rotate, moves, order = tables(angles, cycles)
    chunk = angles // CHUNKS
    wide = chunk + PAD
    forward_high, forward_low = split_table(forward.T)
    rotate_high, rotate_low = split_table(rotate)
    rows = -(-devices * mics // 128) * 128
    theta = 2.0 * np.pi * np.arange(16) / 360.0
    spin = order[:, None] * theta[None, :]
    turns = np.concatenate([np.cos(spin), np.sin(spin)], 0)
    moving = np.zeros((128, 4 * angles), np.float32).astype(BF16)
    for axis in range(2):
        found = three(moves[axis][:, 0])
        for number, piece in enumerate(found):
            start = 48 * axis + 16 * number
            moving[start : start + 2 * SHIFT + 1, axis * 2 * angles :][:, : 2 * angles] = piece
    pieces = three(turns)
    constants = (
        moving,
        np.concatenate(pieces + [np.zeros_like(pieces[0])], 1),
        np.stack([forward_high, forward_low]),
        np.concatenate([forward_high[:, :angles], forward_low[:, :angles]], 1),
        np.stack([rotate_high.T, rotate_low.T]),
        np.concatenate(
            [rotate_high, rotate_low, rotate_high, np.zeros((2 * angles, 8), BF16)], 1
        ),
    )
    sums = jax.ShapeDtypeStruct((1, cycles, 2 * angles), F32)
    dma = pltpu.SemaphoreType.DMA
    scored = pl.pallas_call(
        functools.partial(fused_kernel, (devices, count, cycles, angles)),
        out_shape=(
            jax.ShapeDtypeStruct((classes, count), F32),
            jax.ShapeDtypeStruct((1, count), F32),
            jax.ShapeDtypeStruct((angles, depth), F32),
        ),
        in_specs=[VMEM] * 3 + [pl.BlockSpec(memory_space=pl.ANY)] + [VMEM] * 9,
        out_specs=(VMEM,) * 3,
        scratch_shapes=[
            pltpu.VMEM(particles.shape, BF16),
            dma,
            pltpu.VMEM((devices, mics * cycles, angles), BF16),
            pltpu.VMEM((devices, angles, depth), BF16),
            pltpu.VMEM((angles, depth), BF16),
            pltpu.VMEM((2 * cycles * (count + PAD), angles), F32),
            pltpu.VMEM((rows * (cycles + PAD), angles), F32),
            pltpu.VMEM((4, count, angles), F32),
            pltpu.VMEM((angles * (depth + PAD), count), F32),
            pltpu.VMEM((angles * (2 * classes + PAD), count), F32),
            pltpu.VMEM((2 * classes * (angles + PAD), count), F32),
            pltpu.VMEM((CHUNKS, classes * wide, depth), F32),
            pltpu.VMEM((CHUNKS, classes // 2 * wide, depth), F32),
            pltpu.VMEM((CHUNKS, layers, chunk, depth), F32),
            pltpu.VMEM((CHUNKS, layers, chunk, depth), F32),
            pltpu.VMEM((CHUNKS, layers, chunk, depth), F32),
            pltpu.VMEM((CHUNKS, layers, chunk, depth), F32),
            dma((devices,)),
            dma((devices,)),
            dma((devices,)),
            dma((devices,)),
            dma((2, CHUNKS)),
            dma((2, CHUNKS)),
            dma((2, CHUNKS, layers)),
        ],
        compiler_params=pltpu.CompilerParams(
            collective_id=2, has_side_effects=True, vmem_limit_bytes=60 * MIB
        ),
    )(owner.reshape(1, count), mic_local.reshape(1, count), shifts.T, particles, ctf.reshape(mics * cycles, angles), refs,
      prior.reshape(1, count), *[jnp.asarray(constant) for constant in constants])
    post, evidence, numer, denom = pl.pallas_call(
        finish_kernel,
        out_shape=(
            jax.ShapeDtypeStruct((classes, count), F32),
            jax.ShapeDtypeStruct((1, count), F32),
            sums,
            sums,
        ),
        in_specs=[VMEM] * 3,
        out_specs=(VMEM,) * 4,
        compiler_params=pltpu.CompilerParams(vmem_limit_bytes=60 * MIB),
    )(*scored)
    return post.T, evidence[0], numer, denom


def per_device(particles, owner, mic_local, shifts, prior, refs, ctf):
    devices = lax.axis_size("blk")
    count, cycles, angles = particles.shape[0], particles.shape[1], particles.shape[2] // 2
    local = refs.shape[0]
    classes = local * devices
    mics = ctf.shape[0]
    if local == 1 and classes <= 32:
        return run_fused(particles, owner, mic_local, shifts, prior, refs, ctf, devices)
    forward, rotate, moves, order = tables(angles, cycles)

    values = refs.astype(F32)
    table = jnp.asarray(forward.astype(np.float32))
    spectra = jnp.matmul(values, table, precision=HIGH).astype(BF16)
    power = values[..., :angles] ** 2 + values[..., angles:] ** 2
    power_spectra = jnp.matmul(power, table[:angles], precision=HIGH).astype(BF16)
    both = jnp.stack([spectra, -0.5 * power_spectra], 1).reshape(local, 2, cycles, 2, angles)
    both = both.transpose(0, 4, 3, 1, 2).reshape(local * angles, 4 * cycles)
    own = jnp.concatenate([ctf.reshape(mics * cycles, angles), both.astype(BF16)], 0)
    everything = gather_blocks(own, devices)

    index = jnp.stack([owner[:, 0], mic_local, shifts[:, 0], shifts[:, 1]])
    theta = 2.0 * jnp.pi * prior.astype(F32) / 360.0
    spin = jnp.asarray(order.astype(np.float32))[:, None] * theta[None, :]
    turn = jnp.concatenate([jnp.cos(spin), jnp.sin(spin)], 0)
    forward_t = jnp.asarray(np.stack(split_table(forward.T)))
    rotate_high, rotate_low = split_table(rotate)
    rotate_t = jnp.asarray(np.stack([rotate_high.T, rotate_low.T]))
    spread = jnp.asarray(
        np.concatenate(
            [rotate_high, rotate_low, rotate_high, np.zeros((2 * angles, 8), BF16)], 1
        )
    )
    post, evidence, parts = pl.pallas_call(
        functools.partial(score_kernel, (count, cycles, angles, classes, mics)),
        out_shape=(
            jax.ShapeDtypeStruct((classes, count), F32),
            jax.ShapeDtypeStruct((1, count), F32),
            jax.ShapeDtypeStruct((2 * classes * angles, 4 * cycles), F32),
        ),
        in_specs=[SMEM] + [VMEM] * 8,
        out_specs=(VMEM, VMEM, VMEM),
        scratch_shapes=[
            pltpu.VMEM((3 * cycles * count, angles), F32),
            pltpu.VMEM((angles * 4 * cycles, count), F32),
            pltpu.VMEM((2 * classes * angles, count), F32),
        ],
        compiler_params=pltpu.CompilerParams(vmem_limit_bytes=63 * MIB),
    )(index, particles, everything, jnp.asarray(moves[0], F32), jnp.asarray(moves[1], F32), turn,
      forward_t, rotate_t, spread)
    numer, denom = reduce_blocks(parts[: classes * angles], devices, local, cycles, angles)
    return post.T, evidence[0], numer, denom


def solution(mesh):
    in_specs = (
        P(("groups", "blk"), None, None),
        P(("groups", "blk"), None),
        P(("groups", "blk")),
        P(("groups", "blk"), None),
        P(("groups", "blk")),
        P(("groups", "blk"), None, None),
        P(("groups", "blk"), None, None),
    )
    out_specs = (
        P(("groups", "blk"), None),
        P(("groups", "blk")),
        P(("groups", "blk"), None, None),
        P(("groups", "blk"), None, None),
    )
    return jax.shard_map(
        per_device, mesh=mesh, in_specs=in_specs, out_specs=out_specs, check_vma=False
    )
```

```python
import functools

import jax
import jax.numpy as jnp
import numpy as np
from jax import lax
from jax.experimental import pallas as pl
from jax.experimental.pallas import tpu as pltpu
from jax.sharding import PartitionSpec as P

BOX = 128
ROTS = 36
ROWS = 40
SHIFT = 5
HIGH = lax.Precision.HIGHEST
MESH = pl.DeviceIdType.MESH
F32 = jnp.float32
BF16 = jnp.bfloat16
VMEM = pl.BlockSpec(memory_space=pltpu.VMEM)
SMEM = pl.BlockSpec(memory_space=pltpu.SMEM)
MIB = 1 << 20
PAD = 8
CHUNKS = 2


def split_table(table):
    high = table.astype(np.float32).astype(BF16)
    low = (table - high.astype(np.float64)).astype(np.float32).astype(BF16)
    return high, low


def tables(angles, cycles):
    sample = np.arange(angles)
    order = np.where(sample < angles // 2, sample, sample - angles)
    phase = 2.0 * np.pi * ((sample[:, None] * order[None, :]) % angles) / angles
    cosine, sine = np.cos(phase), np.sin(phase)
    forward = np.block([[cosine, -sine], [sine, cosine]])
    spin = 2.0 * np.pi * ((order[:, None] * np.arange(ROTS)[None, :]) % ROTS) / ROTS
    rotate = np.zeros((2 * angles, ROWS))
    rotate[:, :ROTS] = np.concatenate([np.cos(spin), np.sin(spin)], 0)
    azimuth = 2.0 * np.pi * sample / angles
    step = np.arange(-SHIFT, SHIFT + 1)[:, None, None] * np.arange(1, cycles + 1)[None, :, None]
    moves = []
    for part in (np.cos(azimuth), np.sin(azimuth)):
        turn = -2.0 * np.pi / BOX * step * part[None, None, :]
        moves.append(np.concatenate([np.cos(turn), np.sin(turn)], -1))
    return forward, rotate, moves, order


def neighbours(devices):
    me = lax.axis_index("blk")
    core = lax.rem(me, 2)
    side = lax.rem(me // 2, 2)
    layer = me // 4
    return me, core, side, layer, devices // 4


def greet(partners):
    barrier = pltpu.get_barrier_semaphore()
    for partner in partners:
        pl.semaphore_signal(barrier, inc=1, device_id={"blk": partner}, device_id_type=MESH)
    pl.semaphore_wait(barrier, len(partners))


def gather_kernel(devices, own_ref, all_ref, send_sem, recv_sem):
    me, core, side, layer, layers = neighbours(devices)
    column = side * 2 + core
    across = (1 - side) * 2 + core
    sibling = me + 1 - 2 * core
    beside = me + 2 - 4 * side
    others = [lax.rem(layer + hop, layers) for hop in range(1, layers)]
    greet([other * 4 + column for other in others] + [sibling, beside])
    sent = []

    def send(source, block, target, slot):
        copy = pltpu.make_async_remote_copy(
            src_ref=source,
            dst_ref=all_ref.at[block],
            send_sem=send_sem.at[slot],
            recv_sem=recv_sem.at[block],
            device_id={"blk": target},
            device_id_type=MESH,
        )
        copy.start()
        sent.append(copy)

    def arrive(block):
        pltpu.make_async_remote_copy(
            src_ref=own_ref,
            dst_ref=all_ref.at[block],
            send_sem=send_sem.at[0],
            recv_sem=recv_sem.at[block],
            device_id={"blk": sibling},
            device_id_type=MESH,
        ).wait_recv()

    for hop, other in enumerate(others):
        send(own_ref, me, other * 4 + column, hop)
    send(own_ref, me, beside, layers)
    send(own_ref, me, sibling, 2 * layers)
    all_ref[me] = own_ref[...]
    far = me + 2 - 4 * side
    for hop in range(layers):
        if hop > 0:
            block = others[hop - 1] * 4 + column
            arrive(block)
            send(all_ref.at[block], block, beside, layers + hop)
            send(all_ref.at[block], block, sibling, 2 * layers + hop)
        far = (layer if hop == 0 else others[hop - 1]) * 4 + across
        arrive(far)
        send(all_ref.at[far], far, sibling, 3 * layers + hop)
    for hop in range(layers):
        place = (layer if hop == 0 else others[hop - 1]) * 4
        arrive(place + side * 2 + 1 - core)
        arrive(place + (1 - side) * 2 + 1 - core)
    for copy in sent:
        copy.wait_send()


def gather_blocks(own, devices):
    return pl.pallas_call(
        functools.partial(gather_kernel, devices),
        out_shape=jax.ShapeDtypeStruct((devices,) + own.shape, own.dtype),
        in_specs=[VMEM],
        out_specs=VMEM,
        scratch_shapes=[
            pltpu.SemaphoreType.DMA((devices,)),
            pltpu.SemaphoreType.DMA((devices,)),
        ],
        compiler_params=pltpu.CompilerParams(
            collective_id=0, has_side_effects=True, vmem_limit_bytes=48 * MIB
        ),
    )(own)


def reduce_kernel(devices, local, part_ref, numer_ref, denom_ref, *scratch):
    near, side_in, layer_in, side_out, layer_out, send_sem, near_sem, side_sem, layer_sem = scratch
    me, core, side, layer, layers = neighbours(devices)
    column = side * 2 + core
    sibling = me + 1 - 2 * core
    beside = me + 2 - 4 * side
    depth = part_ref.shape[0] // devices
    others = [lax.rem(layer + hop, layers) for hop in range(1, layers)]
    hops = list(range(1, layers)) + [0]
    greet([other * 4 + column for other in others] + [sibling, beside])

    def rows(block):
        return pl.ds(pl.multiple_of(block * depth, depth), depth)

    def target(hop):
        return layer if hop == 0 else others[hop - 1]

    def copy_to(source, sink, number, sem, device):
        return pltpu.make_async_remote_copy(
            src_ref=source,
            dst_ref=sink,
            send_sem=send_sem.at[number],
            recv_sem=sem,
            device_id={"blk": device},
            device_id_type=MESH,
        )

    first, second, third = {}, {}, {}
    for hop in hops:
        for flip in (1, 0):
            place = jnp.where(side == 1, 1 - flip, flip) if flip else side
            block = target(hop) * 4 + place * 2 + 1 - core
            slot = 2 * hop + flip
            first[slot] = copy_to(
                part_ref.at[rows(block)], near.at[slot], slot, near_sem.at[slot], sibling
            )
            first[slot].start()
    for hop in hops:
        first[2 * hop + 1].wait_recv()
        block = target(hop) * 4 + (1 - side) * 2 + core
        side_out[hop] = part_ref[rows(block), :] + near[2 * hop + 1]
        second[hop] = copy_to(
            side_out.at[hop], side_in.at[hop], 2 * layers + hop, side_sem.at[hop], beside
        )
        second[hop].start()
    for hop in hops:
        first[2 * hop].wait_recv()
        second[hop].wait_recv()
        block = target(hop) * 4 + column
        layer_out[hop] = part_ref[rows(block), :] + near[2 * hop] + side_in[hop]
        if hop:
            third[hop] = copy_to(
                layer_out.at[hop],
                layer_in.at[hop],
                3 * layers + hop,
                layer_sem.at[hop],
                target(hop) * 4 + column,
            )
            third[hop].start()
    total = layer_out[0]
    for hop in range(1, layers):
        third[hop].wait_recv()
        total = total + layer_in[hop]
    cycles, angles = numer_ref.shape[1], numer_ref.shape[2] // 2
    for item in range(local):
        turned = total[item * angles : (item + 1) * angles].T
        numer_ref[item, :, :angles] = turned[:cycles]
        denom_ref[item, :, :angles] = turned[cycles : 2 * cycles]
        numer_ref[item, :, angles:] = turned[2 * cycles : 3 * cycles]
        denom_ref[item, :, angles:] = turned[3 * cycles :]
    for copies in (first, second, third):
        for copy in copies.values():
            copy.wait_send()


def reduce_blocks(parts, devices, local, cycles, angles):
    layers = devices // 4
    depth = local * angles
    lanes = parts.shape[1]
    shape = jax.ShapeDtypeStruct((local, cycles, 2 * angles), F32)
    return pl.pallas_call(
        functools.partial(reduce_kernel, devices, local),
        out_shape=(shape, shape),
        in_specs=[VMEM],
        out_specs=(VMEM, VMEM),
        scratch_shapes=[
            pltpu.VMEM((2 * layers, depth, lanes), F32),
            pltpu.VMEM((layers, depth, lanes), F32),
            pltpu.VMEM((layers, depth, lanes), F32),
            pltpu.VMEM((layers, depth, lanes), F32),
            pltpu.VMEM((layers, depth, lanes), F32),
            pltpu.SemaphoreType.DMA((4 * layers,)),
            pltpu.SemaphoreType.DMA((2 * layers,)),
            pltpu.SemaphoreType.DMA((layers,)),
            pltpu.SemaphoreType.DMA((layers,)),
        ],
        compiler_params=pltpu.CompilerParams(
            collective_id=1, has_side_effects=True, vmem_limit_bytes=48 * MIB
        ),
    )(parts)


def halves(value):
    high = value.astype(BF16)
    return high, (value - high.astype(F32)).astype(BF16)


def dot(left, right):
    return jnp.dot(left, right, preferred_element_type=F32)


def dot_nt(left, right):
    return lax.dot_general(left, right, (((1,), (1,)), ((), ())), preferred_element_type=F32)


def score_kernel(sizes, index_ref, images_ref, all_ref, move_x_ref, move_y_ref, turn_ref,
                 forward_ref, rotate_ref, spread_ref, post_ref, evid_ref, parts_ref,
                 work, spec, refs):
    count, cycles, angles, classes, mics = sizes
    depth = 4 * cycles
    plane = cycles * count

    def shift_one(i):
        own, mic = index_ref[0, i], index_ref[1, i]
        move_x, move_y = move_x_ref[index_ref[2, i] + SHIFT], move_y_ref[index_ref[3, i] + SHIFT]
        row = pl.multiple_of(mic * cycles, cycles)
        transfer = all_ref[own, pl.ds(row, cycles), :].astype(F32)
        image = images_ref[i].astype(F32)
        x_re, x_im = move_x[:, :angles], move_x[:, angles:]
        y_re, y_im = move_y[:, :angles], move_y[:, angles:]
        re = x_re * y_re - x_im * y_im
        im = x_re * y_im + x_im * y_re
        a_re, a_im = image[:, :angles], image[:, angles:]
        work[pl.ds(i, cycles, stride=count), :] = transfer * (a_re * re - a_im * im)
        work[pl.ds(plane + i, cycles, stride=count), :] = transfer * (a_re * im + a_im * re)
        work[pl.ds(2 * plane + i, cycles, stride=count), :] = transfer * transfer

    @pl.loop(0, count // 4)
    def _(group):
        for u in range(4):
            shift_one(group * 4 + u)

    def place_ref(k):
        base = mics * cycles
        half = all_ref[k // sizes_local, pl.ds(base + (k % sizes_local) * angles, angles), :]
        value = half.astype(F32)
        lane = lax.broadcasted_iota(jnp.int32, value.shape, 1)
        swapped = pltpu.roll(value, depth // 2, 1)
        swapped = jnp.where(lane < depth // 2, swapped, -swapped)
        refs[pl.ds(k, angles, stride=2 * classes), :] = value
        refs[pl.ds(classes + k, angles, stride=2 * classes), :] = swapped

    sizes_local = classes // all_ref.shape[0]

    @pl.loop(0, classes // 2)
    def _(group):
        for u in range(2):
            place_ref(group * 2 + u)

    turn_re, turn_im = turn_ref[:angles], turn_ref[angles:]

    def put(values, start):
        re, im = values[:angles], values[angles:]
        spec[pl.ds(start, angles, stride=depth), :] = re * turn_re - im * turn_im
        spec[pl.ds(2 * cycles + start, angles, stride=depth), :] = re * turn_im + im * turn_re

    def transform(p):
        rows = pl.ds(pl.multiple_of(p * count, count), count)
        re = work[rows, :]
        im = work[pl.ds(pl.multiple_of(plane + p * count, count), count), :]
        power = work[pl.ds(pl.multiple_of(2 * plane + p * count, count), count), :]
        high, low = halves(jnp.concatenate([re, im], 1))
        f_high, f_low = forward_ref[0], forward_ref[1]
        values = dot_nt(f_high, high) + dot_nt(f_low, high) + dot_nt(f_high, low)
        put(values, p)
        high, low = halves(power)
        f_high, f_low = f_high[:, :angles], f_low[:, :angles]
        values = dot_nt(f_high, high) + dot_nt(f_low, high) + dot_nt(f_high, low)
        put(values, cycles + p)

    @pl.loop(0, cycles // 2)
    def _(group):
        for u in range(2):
            transform(group * 2 + u)

    def correlate(m):
        held = spec[pl.ds(pl.multiple_of(m * depth, depth), depth), :].astype(BF16)
        rows = pl.ds(pl.multiple_of(m * 2 * classes, 2 * classes), 2 * classes)
        parts_ref[pl.ds(m, 2 * classes, stride=angles), :] = dot(refs[rows, :].astype(BF16), held)

    @pl.loop(0, angles // 8)
    def _(group):
        for u in range(8):
            correlate(group * 8 + u)

    scale = 1.0 / angles
    valid = lax.broadcasted_iota(jnp.int32, (ROWS, count), 0) < ROTS

    def score(k, peak):
        re = parts_ref[pl.ds(pl.multiple_of(k * angles, angles), angles), :]
        im = parts_ref[pl.ds(pl.multiple_of((classes + k) * angles, angles), angles), :]
        high, low = halves(jnp.concatenate([re, im], 0))
        r_high, r_low = rotate_ref[0], rotate_ref[1]
        value = (dot(r_high, high) + dot(r_low, high) + dot(r_high, low)) * scale
        value = jnp.where(valid, value, -jnp.inf)
        work[pl.ds(pl.multiple_of(k * ROWS, 8), ROWS), :] = value
        return jnp.maximum(peak, value)

    def score_two(group, peak):
        return score(group * 2 + 1, score(group * 2, peak))

    peak = lax.fori_loop(0, classes // 2, score_two, jnp.full((ROWS, count), -jnp.inf, F32))
    peak = jnp.max(peak, axis=0, keepdims=True)

    def expo(k, total):
        rows = pl.ds(pl.multiple_of(k * ROWS, 8), ROWS)
        value = jnp.exp(work[rows, :] - peak)
        work[rows, :] = value
        return total + value

    total = lax.fori_loop(0, classes, expo, jnp.zeros((ROWS, count), F32))
    total = jnp.sum(total, axis=0, keepdims=True)
    evid_ref[...] = peak + jnp.log(total)
    share = 1.0 / total

    def unrotate(k):
        weights = work[pl.ds(pl.multiple_of(k * ROWS, 8), ROWS), :] * share
        post_ref[pl.ds(k, 1), :] = jnp.sum(weights, axis=0, keepdims=True)
        high, low = halves(weights)
        stacked = jnp.concatenate(
            [high.astype(F32), high.astype(F32), low.astype(F32), jnp.zeros((8, count), F32)], 0
        ).astype(BF16)
        value = dot(spread_ref[...], stacked)
        refs[pl.ds(k, angles, stride=2 * classes), :] = value[:angles]
        refs[pl.ds(classes + k, angles, stride=2 * classes), :] = value[angles:]

    @pl.loop(0, classes // 2)
    def _(group):
        for u in range(2):
            unrotate(group * 2 + u)

    def gather_up(m):
        held = spec[pl.ds(pl.multiple_of(m * depth, depth), depth), :]
        other = jnp.concatenate([-held[depth // 2 :], held[: depth // 2]], 0)
        right = jnp.concatenate([held, other], 1).astype(BF16)
        rows = pl.ds(pl.multiple_of(m * 2 * classes, 2 * classes), 2 * classes)
        spun = refs[rows, :]
        left = jnp.concatenate([spun[:classes], spun[classes:]], 1).astype(BF16)
        parts_ref[pl.ds(m, classes, stride=angles), :] = dot_nt(left, right)

    @pl.loop(0, angles // 8)
    def _(group):
        for u in range(8):
            gather_up(group * 8 + u)


def fused_kernel(sizes, owner_ref, mic_ref, shift_ref, particles_ref, ctf_ref, own_values_ref,
                 prior_ref, moves_ref, turns_ref, forward_ref, power_ref,
                 rotate_ref, spread_ref, post_ref, evid_ref, total_ref,
                 images_ref, images_sem, all_ctf, all_refs, own_refs, work, table, phase, spec, refs, mixed, parts,
                 near, side_out, side_in, layer_out, layer_in,
                 ctf_send, ctf_recv, refs_send, refs_recv, near_sems, side_sems, layer_sems):
    devices, count, cycles, angles = sizes
    classes = devices
    depth = 4 * cycles
    lane_rows, deep, pairs, tall = count + PAD, depth + PAD, 2 * classes + PAD, angles + PAD
    plane = cycles * lane_rows
    chunk = angles // CHUNKS
    wide = chunk + PAD

    fetch = pltpu.make_async_copy(particles_ref, images_ref, images_sem)
    fetch.start()
    me, core, side, layer, layers = neighbours(devices)
    column = side * 2 + core
    sibling = me + 1 - 2 * core
    beside = me + 2 - 4 * side
    others = [lax.rem(layer + hop, layers) for hop in range(1, layers)]
    places = [layer] + others
    greet([other * 4 + column for other in others] + [sibling, beside])
    waiting = []

    def push(source, sink, send_sem, recv_sem, device):
        copy = pltpu.make_async_remote_copy(
            src_ref=source,
            dst_ref=sink,
            send_sem=send_sem,
            recv_sem=recv_sem,
            device_id={"blk": device},
            device_id_type=MESH,
        )
        copy.start()
        waiting.append(copy)
        return copy

    def spreader(own, everything, sends, recvs):
        def send(source, block, device, slot):
            push(source, everything.at[block], sends.at[slot], recvs.at[block], device)

        def arrive(block):
            pltpu.make_async_remote_copy(
                src_ref=own,
                dst_ref=everything.at[block],
                send_sem=sends.at[0],
                recv_sem=recvs.at[block],
                device_id={"blk": sibling},
                device_id_type=MESH,
            ).wait_recv()

        def begin():
            for hop, other in enumerate(others):
                send(own, me, other * 4 + column, hop)
            send(own, me, beside, layers)
            send(own, me, sibling, 2 * layers)

        def along(hop):
            block = places[hop] * 4 + column
            arrive(block)
            send(everything.at[block], block, beside, layers + hop)
            send(everything.at[block], block, sibling, 2 * layers + hop)

        def over(hop):
            block = places[hop] * 4 + (1 - side) * 2 + core
            arrive(block)
            send(everything.at[block], block, sibling, 3 * layers + hop)

        def finish():
            for place in places:
                arrive(place * 4 + side * 2 + 1 - core)
                arrive(place * 4 + (1 - side) * 2 + 1 - core)

        return begin, along, over, finish

    ctf_begin, ctf_along, ctf_over, ctf_finish = spreader(ctf_ref, all_ctf, ctf_send, ctf_recv)
    refs_begin, refs_along, refs_over, refs_finish = spreader(
        own_refs, all_refs, refs_send, refs_recv
    )

    ctf_begin()
    all_ctf[me] = ctf_ref[...]
    f_high, f_low = forward_ref[0], forward_ref[1]
    values = own_values_ref[0].astype(F32)
    v_re, v_im = values[:, :angles], values[:, angles:]
    halved = -0.5 * (v_re * v_re + v_im * v_im)
    none = jnp.zeros_like(halved)
    stacked = jnp.concatenate(
        [
            values,
            jnp.concatenate([halved, none], 1),
            jnp.concatenate([v_im, -v_re], 1),
            jnp.concatenate([none, -halved], 1),
        ],
        0,
    )
    high, low = halves(stacked)
    top, bottom = f_high[:angles], f_low[:angles]
    own_block = (dot_nt(top, high) + dot_nt(bottom, high) + dot_nt(top, low)).astype(BF16)
    own_refs[...] = own_block
    all_refs[me] = own_block
    refs_begin()
    table[...] = jnp.zeros_like(table)
    parts[...] = jnp.zeros_like(parts)
    fetch.wait()

    def spread_image(i):
        image = images_ref[i].astype(F32)
        work[pl.ds(i, cycles, stride=lane_rows), :] = image[:, :angles]
        work[pl.ds(plane + i, cycles, stride=lane_rows), :] = image[:, angles:]

    def picks(rows, line):
        return (lax.broadcasted_iota(jnp.int32, (rows, count), 0) == line).astype(F32)

    step_x, step_y = picks(16, shift_ref[0:1] + SHIFT), picks(16, shift_ref[1:2] + SHIFT)
    blank = jnp.zeros((32, count), F32)
    moved = jnp.concatenate([step_x] * 3 + [step_y] * 3 + [blank], 0).T.astype(BF16)
    moved = dot(moved, moves_ref[...])
    x_re, x_im = moved[:, :angles], moved[:, angles : 2 * angles]
    y_re, y_im = moved[:, 2 * angles : 3 * angles], moved[:, 3 * angles :]
    for slot in (0, 2):
        phase[slot] = x_re * y_re - x_im * y_im
        phase[slot + 1] = x_re * y_im + x_im * y_re
    mics = ctf_ref.shape[0] // cycles
    held_rows = table.shape[0] // (cycles + PAD)
    picked = picks(held_rows, owner_ref[...] * mics + mic_ref[...]).T.astype(BF16)

    chosen = picks(16, prior_ref[...])
    chosen = jnp.concatenate([chosen, chosen, chosen, jnp.zeros_like(chosen)], 0).astype(BF16)
    turn = dot(turns_ref[...], chosen)
    turn_re, turn_im = turn[:angles], turn[angles:]
    steps = max(layers, 1)
    span = count // steps

    for hop in range(steps):

        @pl.loop(0, span // 4)
        def _(group):
            for u in range(4):
                spread_image(hop * span + group * 4 + u)

        if hop + 1 < layers:
            ctf_along(hop + 1)
    for hop in range(layers):
        ctf_over(hop)
    ctf_finish()

    @pl.loop(0, devices)
    def _(block):
        for mic in range(mics):
            row = pl.multiple_of((block * mics + mic) * (cycles + PAD), 8)
            rows = all_ctf[block, mic * cycles : (mic + 1) * cycles, :]
            table[pl.ds(row, cycles), :] = rows.astype(F32)

    def put(values, start):
        re, im = values[:angles], values[angles:]
        spec[pl.ds(start, angles, stride=deep), :] = re * turn_re - im * turn_im
        spec[pl.ds(2 * cycles + start, angles, stride=deep), :] = re * turn_im + im * turn_re

    def transform(p):
        lines, powers = [], []
        w_re, w_im = phase[2], phase[3]
        t_re, t_im = phase[0], phase[1]
        for u in range(2):
            row = pl.multiple_of((p + u) * lane_rows, 8)
            scale = dot(picked, table[pl.ds(p + u, held_rows, stride=cycles + PAD), :].astype(BF16))
            a_re = work[pl.ds(row, count), :] * scale
            a_im = work[pl.ds(pl.multiple_of(plane + (p + u) * lane_rows, 8), count), :] * scale
            re, im = a_re * t_re - a_im * t_im, a_re * t_im + a_im * t_re
            t_re, t_im = t_re * w_re - t_im * w_im, t_re * w_im + t_im * w_re
            lines.append(jnp.concatenate([re, im], 1))
            powers.append(scale * scale)
        phase[0] = t_re
        phase[1] = t_im
        high, low = halves(jnp.concatenate(lines, 0))
        values = dot_nt(forward_ref[0], high) + dot_nt(forward_ref[1], high)
        values = values + dot_nt(forward_ref[0], low)
        put(values[:, :count], p)
        put(values[:, count:], p + 1)
        high, low = halves(jnp.concatenate(powers, 0))
        both = power_ref[...]
        values = dot_nt(both, jnp.concatenate([high, high], 1))
        values = values + dot_nt(both[:, :angles], low)
        put(values[:, :count], cycles + p)
        put(values[:, count:], cycles + p + 1)

    part = cycles // steps
    for hop in range(steps):

        @pl.loop(0, part // 2)
        def _(group):
            transform(hop * part + group * 2)

        if hop == 0:
            for other in range(1, layers):
                refs_along(other)
        if hop == max(steps - 2, 0):
            for other in range(layers // 2):
                refs_over(other)
    for other in range(layers // 2, layers):
        refs_over(other)
    refs_finish()

    def position(k):
        return (k % 2) * (classes // 2) + ((k // 2) % 2) * (classes // 4) + k // 4

    def place_ref(k):
        value = all_refs[k].astype(F32)
        lane = lax.broadcasted_iota(jnp.int32, value.shape, 1)
        swapped = pltpu.roll(value, depth // 2, 1)
        swapped = jnp.where(lane < depth // 2, swapped, -swapped)
        refs[pl.ds(position(k), angles, stride=pairs), :] = value
        refs[pl.ds(classes + position(k), angles, stride=pairs), :] = swapped

    @pl.loop(0, classes // 2)
    def _(group):
        for u in range(2):
            place_ref(group * 2 + u)

    def correlate(m):
        held = spec[pl.ds(pl.multiple_of(m * deep, 8), depth), :].astype(BF16)
        rows = pl.ds(pl.multiple_of(m * pairs, 8), 2 * classes)
        mixed[pl.ds(m, 2 * classes, stride=tall), :] = dot(refs[rows, :].astype(BF16), held)

    @pl.loop(0, angles // 8)
    def _(group):
        for u in range(8):
            correlate(group * 8 + u)

    valid = lax.broadcasted_iota(jnp.int32, (ROWS, count), 0) < ROTS

    def score(k, peak):
        re = mixed[pl.ds(pl.multiple_of(k * tall, 8), angles), :]
        im = mixed[pl.ds(pl.multiple_of((classes + k) * tall, 8), angles), :]
        high, low = halves(jnp.concatenate([re, im], 0))
        r_high, r_low = rotate_ref[0], rotate_ref[1]
        value = (dot(r_high, high) + dot(r_low, high) + dot(r_high, low)) * (1.0 / angles)
        value = jnp.where(valid, value, -jnp.inf)
        work[pl.ds(pl.multiple_of(k * ROWS, 8), ROWS), :] = value
        return jnp.maximum(peak, value)

    def score_four(group, peak):
        for u in range(4):
            peak = score(group * 4 + u, peak)
        return peak

    peak = lax.fori_loop(0, classes // 4, score_four, jnp.full((ROWS, count), -jnp.inf, F32))
    peak = jnp.max(peak, axis=0, keepdims=True)

    def expo(k, total):
        rows = pl.ds(pl.multiple_of(k * ROWS, 8), ROWS)
        value = jnp.exp(work[rows, :] - peak)
        work[rows, :] = value
        return total + value

    total = lax.fori_loop(0, classes, expo, jnp.zeros((ROWS, count), F32))
    total = jnp.sum(total, axis=0, keepdims=True)
    evid_ref[...] = peak + jnp.log(total)
    share = 1.0 / total

    def unrotate(k):
        row = position(k)
        weights = work[pl.ds(pl.multiple_of(row * ROWS, 8), ROWS), :] * share
        post_ref[pl.ds(k, 1), :] = jnp.sum(weights, axis=0, keepdims=True)
        high, low = halves(weights)
        stacked = jnp.concatenate(
            [high.astype(F32), high.astype(F32), low.astype(F32), jnp.zeros((8, count), F32)], 0
        ).astype(BF16)
        value = dot(spread_ref[...], stacked)
        refs[pl.ds(row, angles, stride=pairs), :] = value[:angles]
        refs[pl.ds(classes + row, angles, stride=pairs), :] = value[angles:]

    @pl.loop(0, classes // 4)
    def _(group):
        for u in range(4):
            unrotate(group * 4 + u)

    def gather_up(number, step):
        m = number * chunk + step
        held = spec[pl.ds(pl.multiple_of(m * deep, 8), depth), :]
        other = jnp.concatenate([-held[depth // 2 :], held[: depth // 2]], 0)
        right = jnp.concatenate([held, other], 1).astype(BF16)
        spun = refs[pl.ds(pl.multiple_of(m * pairs, 8), 2 * classes), :]
        left = jnp.concatenate([spun[:classes], spun[classes:]], 1).astype(BF16)
        parts.at[number][pl.ds(step, classes, stride=wide), :] = dot_nt(left, right)

    half, quarter = classes // 2 * wide, classes // 4 * wide

    def near_rows(number, flip, place):
        place = pl.multiple_of(flip * quarter + place * wide, 8)
        mine = pl.multiple_of(core * half + place, 8)
        return parts[number, pl.ds(mine, chunk), :] + near[number, pl.ds(place, chunk), :]

    first, second, third = {}, {}, {}

    def stage_near(number):
        start = pl.multiple_of((1 - core) * half, 8)
        first[number] = push(
            parts.at[number, pl.ds(start, half)],
            near.at[number],
            near_sems.at[0, number],
            near_sems.at[1, number],
            sibling,
        )

    def stage_side(number):
        first[number].wait_recv()
        for place in range(layers):
            side_out[number, place] = near_rows(number, 1 - side, place)
        second[number] = push(
            side_out.at[number],
            side_in.at[number],
            side_sems.at[0, number],
            side_sems.at[1, number],
            beside,
        )

    def stage_layer(number):
        second[number].wait_recv()
        for hop, place in enumerate(places):
            layer_out[number, hop] = near_rows(number, side, place) + side_in[number, place]
            if hop:
                third[number, hop] = push(
                    layer_out.at[number, hop],
                    layer_in.at[number, hop],
                    layer_sems.at[0, number, hop],
                    layer_sems.at[1, number, hop],
                    place * 4 + column,
                )

    def stage_total(number):
        total = layer_out[number, 0]
        for hop in range(1, layers):
            third[number, hop].wait_recv()
            total = total + layer_in[number, hop]
        return total

    for number in range(CHUNKS):

        @pl.loop(0, chunk // 8)
        def _(group):
            for u in range(8):
                gather_up(number, group * 8 + u)

        stage_near(number)
        if number >= 1:
            stage_side(number - 1)
        if number >= 2:
            stage_layer(number - 2)
    stage_side(CHUNKS - 1)
    if CHUNKS >= 2:
        stage_layer(CHUNKS - 2)
    stage_layer(CHUNKS - 1)
    for number in range(CHUNKS):
        total_ref[number * chunk : (number + 1) * chunk] = stage_total(number)
    for copy in waiting:
        copy.wait_send()


def finish_kernel(post_in, evid_in, total_ref, post_ref, evid_ref, numer_ref, denom_ref):
    cycles, angles = numer_ref.shape[1], numer_ref.shape[2] // 2
    post_ref[...] = post_in[...]
    evid_ref[...] = evid_in[...]
    turned = total_ref[...].T
    numer_ref[0, :, :angles] = turned[:cycles]
    denom_ref[0, :, :angles] = turned[cycles : 2 * cycles]
    numer_ref[0, :, angles:] = turned[2 * cycles : 3 * cycles]
    denom_ref[0, :, angles:] = turned[3 * cycles :]


def three(values):
    pieces = []
    rest = values.astype(np.float64)
    for _ in range(3):
        piece = rest.astype(np.float32).astype(BF16)
        pieces.append(piece)
        rest = rest - piece.astype(np.float64)
    return pieces


def run_fused(particles, owner, mic_local, shifts, prior, refs, ctf, devices):
    count, cycles, angles = particles.shape[0], particles.shape[1], particles.shape[2] // 2
    classes = devices
    layers = devices // 4
    mics = ctf.shape[0]
    depth = 4 * cycles
    forward, rotate, moves, order = tables(angles, cycles)
    chunk = angles // CHUNKS
    wide = chunk + PAD
    forward_high, forward_low = split_table(forward.T)
    rotate_high, rotate_low = split_table(rotate)
    rows = -(-devices * mics // 128) * 128
    theta = 2.0 * np.pi * np.arange(16) / 360.0
    spin = order[:, None] * theta[None, :]
    turns = np.concatenate([np.cos(spin), np.sin(spin)], 0)
    moving = np.zeros((128, 4 * angles), np.float32).astype(BF16)
    for axis in range(2):
        found = three(moves[axis][:, 0])
        for number, piece in enumerate(found):
            start = 48 * axis + 16 * number
            moving[start : start + 2 * SHIFT + 1, axis * 2 * angles :][:, : 2 * angles] = piece
    pieces = three(turns)
    constants = (
        moving,
        np.concatenate(pieces + [np.zeros_like(pieces[0])], 1),
        np.stack([forward_high, forward_low]),
        np.concatenate([forward_high[:, :angles], forward_low[:, :angles]], 1),
        np.stack([rotate_high.T, rotate_low.T]),
        np.concatenate(
            [rotate_high, rotate_low, rotate_high, np.zeros((2 * angles, 8), BF16)], 1
        ),
    )
    sums = jax.ShapeDtypeStruct((1, cycles, 2 * angles), F32)
    dma = pltpu.SemaphoreType.DMA
    scored = pl.pallas_call(
        functools.partial(fused_kernel, (devices, count, cycles, angles)),
        out_shape=(
            jax.ShapeDtypeStruct((classes, count), F32),
            jax.ShapeDtypeStruct((1, count), F32),
            jax.ShapeDtypeStruct((angles, depth), F32),
        ),
        in_specs=[VMEM] * 3 + [pl.BlockSpec(memory_space=pl.ANY)] + [VMEM] * 9,
        out_specs=(VMEM,) * 3,
        scratch_shapes=[
            pltpu.VMEM(particles.shape, BF16),
            dma,
            pltpu.VMEM((devices, mics * cycles, angles), BF16),
            pltpu.VMEM((devices, angles, depth), BF16),
            pltpu.VMEM((angles, depth), BF16),
            pltpu.VMEM((2 * cycles * (count + PAD), angles), F32),
            pltpu.VMEM((rows * (cycles + PAD), angles), F32),
            pltpu.VMEM((4, count, angles), F32),
            pltpu.VMEM((angles * (depth + PAD), count), F32),
            pltpu.VMEM((angles * (2 * classes + PAD), count), F32),
            pltpu.VMEM((2 * classes * (angles + PAD), count), F32),
            pltpu.VMEM((CHUNKS, classes * wide, depth), F32),
            pltpu.VMEM((CHUNKS, classes // 2 * wide, depth), F32),
            pltpu.VMEM((CHUNKS, layers, chunk, depth), F32),
            pltpu.VMEM((CHUNKS, layers, chunk, depth), F32),
            pltpu.VMEM((CHUNKS, layers, chunk, depth), F32),
            pltpu.VMEM((CHUNKS, layers, chunk, depth), F32),
            dma((devices,)),
            dma((devices,)),
            dma((devices,)),
            dma((devices,)),
            dma((2, CHUNKS)),
            dma((2, CHUNKS)),
            dma((2, CHUNKS, layers)),
        ],
        compiler_params=pltpu.CompilerParams(
            collective_id=2, has_side_effects=True, vmem_limit_bytes=60 * MIB
        ),
    )(owner.reshape(1, count), mic_local.reshape(1, count), shifts.T, particles, ctf.reshape(mics * cycles, angles), refs,
      prior.reshape(1, count), *[jnp.asarray(constant) for constant in constants])
    post, evidence, numer, denom = pl.pallas_call(
        finish_kernel,
        out_shape=(
            jax.ShapeDtypeStruct((classes, count), F32),
            jax.ShapeDtypeStruct((1, count), F32),
            sums,
            sums,
        ),
        in_specs=[VMEM] * 3,
        out_specs=(VMEM,) * 4,
        compiler_params=pltpu.CompilerParams(vmem_limit_bytes=60 * MIB),
    )(*scored)
    return post.T, evidence[0], numer, denom


def per_device(particles, owner, mic_local, shifts, prior, refs, ctf):
    devices = lax.axis_size("blk")
    count, cycles, angles = particles.shape[0], particles.shape[1], particles.shape[2] // 2
    local = refs.shape[0]
    classes = local * devices
    mics = ctf.shape[0]
    if local == 1 and classes <= 32:
        return run_fused(particles, owner, mic_local, shifts, prior, refs, ctf, devices)
    forward, rotate, moves, order = tables(angles, cycles)

    values = refs.astype(F32)
    table = jnp.asarray(forward.astype(np.float32))
    spectra = jnp.matmul(values, table, precision=HIGH).astype(BF16)
    power = values[..., :angles] ** 2 + values[..., angles:] ** 2
    power_spectra = jnp.matmul(power, table[:angles], precision=HIGH).astype(BF16)
    both = jnp.stack([spectra, -0.5 * power_spectra], 1).reshape(local, 2, cycles, 2, angles)
    both = both.transpose(0, 4, 3, 1, 2).reshape(local * angles, 4 * cycles)
    own = jnp.concatenate([ctf.reshape(mics * cycles, angles), both.astype(BF16)], 0)
    everything = gather_blocks(own, devices)

    index = jnp.stack([owner[:, 0], mic_local, shifts[:, 0], shifts[:, 1]])
    theta = 2.0 * jnp.pi * prior.astype(F32) / 360.0
    spin = jnp.asarray(order.astype(np.float32))[:, None] * theta[None, :]
    turn = jnp.concatenate([jnp.cos(spin), jnp.sin(spin)], 0)
    forward_t = jnp.asarray(np.stack(split_table(forward.T)))
    rotate_high, rotate_low = split_table(rotate)
    rotate_t = jnp.asarray(np.stack([rotate_high.T, rotate_low.T]))
    spread = jnp.asarray(
        np.concatenate(
            [rotate_high, rotate_low, rotate_high, np.zeros((2 * angles, 8), BF16)], 1
        )
    )
    post, evidence, parts = pl.pallas_call(
        functools.partial(score_kernel, (count, cycles, angles, classes, mics)),
        out_shape=(
            jax.ShapeDtypeStruct((classes, count), F32),
            jax.ShapeDtypeStruct((1, count), F32),
            jax.ShapeDtypeStruct((2 * classes * angles, 4 * cycles), F32),
        ),
        in_specs=[SMEM] + [VMEM] * 8,
        out_specs=(VMEM, VMEM, VMEM),
        scratch_shapes=[
            pltpu.VMEM((3 * cycles * count, angles), F32),
            pltpu.VMEM((angles * 4 * cycles, count), F32),
            pltpu.VMEM((2 * classes * angles, count), F32),
        ],
        compiler_params=pltpu.CompilerParams(vmem_limit_bytes=63 * MIB),
    )(index, particles, everything, jnp.asarray(moves[0], F32), jnp.asarray(moves[1], F32), turn,
      forward_t, rotate_t, spread)
    numer, denom = reduce_blocks(parts[: classes * angles], devices, local, cycles, angles)
    return post.T, evidence[0], numer, denom


def solution(mesh):
    in_specs = (
        P(("groups", "blk"), None, None),
        P(("groups", "blk"), None),
        P(("groups", "blk")),
        P(("groups", "blk"), None),
        P(("groups", "blk")),
        P(("groups", "blk"), None, None),
        P(("groups", "blk"), None, None),
    )
    out_specs = (
        P(("groups", "blk"), None),
        P(("groups", "blk")),
        P(("groups", "blk"), None, None),
        P(("groups", "blk"), None, None),
    )
    return jax.shard_map(
        per_device, mesh=mesh, in_specs=in_specs, out_specs=out_specs, check_vma=False
    )
```
